128 devices in a mesh: xs: 4 (over x), ax: 32 (over y, z, core).
Axes of the slice: x: 4, y: 4, z: 4, core: 2. Of those that a mesh axis runs over, the one named last changes fastest.
Arguments:
- concentration: float32 [1024, 128, 384], P('ax', 'xs'), may hold values from -4 to 4
- tissue_mask: int32 [1024, 128, 384], P('ax', 'xs'), may hold values from 0 to 1
- wall_layer: int32 [1024, 128, 384], P('ax', 'xs'), may hold values from 0 to 3, as said below
- stiffness: float32 [1024, 128, 384], P('ax', 'xs'), may hold values from 1 to 2
- production: float32 [1024, 128, 384], P('ax', 'xs'), may hold values from -3 to 3
- layer_diffusivity: float32 [4], replicated, may hold values from 1 to 2
- uptake_rate: float32 [4], replicated, may hold values from 0.1 to 0.5
Outputs:
- concentration_out: float32 [1024, 128, 384], P('ax', 'xs')
The draws below stay inside these ranges and needn't reach their ends.
Inputs may be any that keep to these rules, and one draw needn't show every extreme that they name: `wall_layer`: indexes the tables of layer coefficients.
All inputs are finite; a program needn't handle non-finite values.
Results may differ from the reference program's by a relative error of at most 0.0003.
Values sent between devices are 32-bit elements; how exact they have to be, the bound alone decides.
No kernel may reach another device: no remote copies, remote signals or barrier semaphores. Data moves between devices by JAX's collectives and lax.ppermute only.
A program may use at most 128 MiB of HBM per device.

```python
import math
import jax
import jax.numpy as jnp
from jax import lax

NY = 384
STEPS = 2
LAYERS = 4
NX = 128
NZ = 1024
RZ = 3072


def wall_geometry(key):
    base_key = jax.random.fold_in(key, 11)
    subkeys = jax.random.split(base_key, 3)
    centre_x = NX // 2 + jax.random.randint(subkeys[0], (), -(NX // 8), NX // 8 + 1)
    centre_y = NY // 2 + jax.random.randint(subkeys[1], (), -(NY // 8), NY // 8 + 1)
    bulge_start = jax.random.randint(subkeys[2], (), 0, NZ - NZ // 4 + 1)
    lumen_radius = NX // 4
    bulge_size = max(NX // 16, 1)
    layer_width = max(NX // 16, 1)
    axial = jnp.arange(NZ, dtype=jnp.int32)[:, None, None]
    across = jnp.arange(NX, dtype=jnp.int32)[None, :, None]
    along_y = jnp.arange(NY, dtype=jnp.int32)[None, None, :]
    inside = ((axial >= bulge_start) & (axial < bulge_start + NZ // 4)).astype(jnp.int32)
    radius = lumen_radius + bulge_size * inside
    radial_sq = (across - centre_x) * (across - centre_x) + (along_y - centre_y) * (along_y - centre_y)
    return (radius, radial_sq, layer_width)


def draw_tissue_mask(key, part):
    radius, radial_sq, layer_width = wall_geometry(key)
    return (radial_sq >= radius * radius).astype(jnp.int32)


def draw_wall_layer(key, part):
    radius, radial_sq, layer_width = wall_geometry(key)
    labels = jnp.zeros(radial_sq.shape, jnp.int32)
    for band_index in range(1, 4):
        edge = radius + band_index * layer_width
        labels = labels + (radial_sq >= edge * edge).astype(jnp.int32)
    return labels


def draw_concentration(key, part):
    base_key = jax.random.fold_in(key, 23)
    return jnp.clip(jax.random.normal(base_key, (NZ, NX, NY), jnp.float32), -4.0, 4.0)


def block_scale(rng, extent, cuts, low, largest):
    factor_of = 1.0
    for axis_at, blocks in cuts:
        heights = jax.random.uniform(jax.random.fold_in(jax.random.fold_in(rng, 6), axis_at), (blocks,), jnp.float32, low / len(cuts), largest / len(cuts))
        factor_of = factor_of * jnp.repeat(jnp.exp(heights), extent[axis_at] // blocks).reshape((-1,) + (1,) * (len(extent) - 1 - axis_at))
    return factor_of


def centred(key, extent, width, limit, cuts=(), held_as=jnp.bfloat16):
    array = jax.random.normal(key, extent, jnp.float32) * width
    if len(cuts) > 0:
        array = block_scale(key, extent, cuts, -0.22, 0.18) * array
    return jnp.clip(array, min=-limit, max=limit).astype(held_as)


def setup_inputs(seed: int = 0) -> dict:
    keys = jax.random.split(jax.random.key(seed), 8)
    return {
        "concentration": draw_concentration(jax.random.fold_in(keys[7], 71), 0),
        "tissue_mask": draw_tissue_mask(jax.random.fold_in(keys[7], 71), 0),
        "wall_layer": draw_wall_layer(jax.random.fold_in(keys[7], 71), 0),
        "stiffness": jnp.clip(jnp.exp(math.log(2.0) - 0.6931472 * jax.random.uniform(keys[3], (NZ, NX, NY), jnp.float32) ** block_scale(keys[3], (NZ, NX, NY), ((0, 32), (1, 4)), -0.2, 0.2)), 1.0, 2.0),
        "production": centred(keys[4], (NZ, NX, NY), 0.5, 3.0, ((0, 32), (1, 4)), jnp.float32),
        "layer_diffusivity": jnp.clip(jnp.exp(jax.random.uniform(keys[5], (LAYERS,), jnp.float32, math.log(1.0), math.log(2.0))), 1.0, 2.0),
        "uptake_rate": jnp.clip(jnp.exp(jax.random.uniform(keys[6], (LAYERS,), jnp.float32, math.log(0.1), math.log(0.5))), 0.1, 0.5),
    }


SECTION_RATE = 0.05

def table_lookup(labels, coeffs):
    summed = jnp.zeros(labels.shape, jnp.float32)
    for layer_index in range(coeffs.shape[0]):
        summed = summed + jnp.where(labels == layer_index, coeffs[layer_index], 0.0)
    return summed

def lower_neighbour(values, axis_id):
    zero_plane = jnp.zeros_like(lax.slice_in_dim(values, 0, 1, axis=axis_id))
    kept = lax.slice_in_dim(values, 0, values.shape[axis_id] - 1, axis=axis_id)
    return jnp.concatenate([zero_plane, kept], axis=axis_id)

def upper_neighbour(values, axis_id):
    zero_plane = jnp.zeros_like(lax.slice_in_dim(values, 0, 1, axis=axis_id))
    kept = lax.slice_in_dim(values, 1, values.shape[axis_id], axis=axis_id)
    return jnp.concatenate([kept, zero_plane], axis=axis_id)

def axial_solve(lower_band, diagonal, upper_band, rhs_vals):

    def forward(carried, row_data):
        prev_ratio, prev_value = carried
        low_coef, diag_coef, high_coef, right_side = row_data
        pivot = diag_coef - low_coef * prev_ratio
        new_ratio = high_coef / pivot
        new_value = (right_side - low_coef * prev_value) / pivot
        return ((new_ratio, new_value), (new_ratio, new_value))
    zero_plane = jnp.zeros(rhs_vals.shape[1:], jnp.float32)
    _, (ratios, values) = lax.scan(forward, (zero_plane, zero_plane), (lower_band, diagonal, upper_band, rhs_vals))

    def backward(next_value, row_data):
        ratio_row, value_row = row_data
        solved_row = value_row - ratio_row * next_value
        return (solved_row, solved_row)
    _, solved = lax.scan(backward, zero_plane, (ratios, values), reverse=True)
    return solved

def reference(concentration, tissue_mask, wall_layer, stiffness, production, layer_diffusivity, uptake_rate):
    tissue_weight = tissue_mask.astype(jnp.float32)
    diffusivity = tissue_weight * table_lookup(wall_layer, layer_diffusivity) * stiffness
    uptake_cell = tissue_weight * table_lookup(wall_layer, uptake_rate)
    source_cell = tissue_weight * production
    weights = []
    for axis_id in range(3):
        weights.append((jnp.sqrt(diffusivity * lower_neighbour(diffusivity, axis_id)), jnp.sqrt(diffusivity * upper_neighbour(diffusivity, axis_id))))
    lower_band = -RZ * weights[0][0]
    upper_band = -RZ * weights[0][1]
    diagonal = 1.0 + RZ * (weights[0][0] + weights[0][1])
    state_now = concentration
    for step_index in range(STEPS):
        net_flux = jnp.zeros_like(state_now)
        for axis_id in (1, 2):
            net_flux = net_flux + weights[axis_id][0] * (lower_neighbour(state_now, axis_id) - state_now)
            net_flux = net_flux + weights[axis_id][1] * (upper_neighbour(state_now, axis_id) - state_now)
        explicit = state_now + SECTION_RATE * net_flux
        solved = axial_solve(lower_band, diagonal, upper_band, explicit)
        state_now = solved + (source_cell - uptake_cell * solved)
    return state_now
```

```python
import functools

import jax
import jax.numpy as jnp
from jax import lax
from jax.experimental import pallas as pl
from jax.experimental.pallas import tpu as pltpu
from jax.sharding import PartitionSpec as P

RZ = 3072.0
SECTION_RATE = 0.05
LAYERS = 4
LIMIT = 20 * 1024 * 1024
CHUNK = 8


def at_vmem(*shape):
    return pltpu.VMEM(shape, jnp.float32)


def vspec():
    return pl.BlockSpec(memory_space=pltpu.VMEM)


def params():
    return pltpu.CompilerParams(vmem_limit_bytes=LIMIT)


def cost(us):
    return pl.CostEstimate(flops=int(us * 2e6), bytes_accessed=int(us * 3e6), transcendentals=0)


def lookup(labels, table):
    summed = jnp.where(labels == 0, table[0], 0.0)
    for layer in range(1, LAYERS):
        summed = jnp.where(labels == layer, table[layer], summed)
    return summed


def neighbour_sum(plane):
    slab, cols = plane.shape
    row = lax.broadcasted_iota(jnp.int32, plane.shape, 0)
    col = lax.broadcasted_iota(jnp.int32, plane.shape, 1)
    below = jnp.where(row == 0, 0.0, pltpu.roll(plane, 1, 0))
    above = jnp.where(row == slab - 1, 0.0, pltpu.roll(plane, slab - 1, 0))
    left = jnp.where(col == 0, 0.0, pltpu.roll(plane, 1, 1))
    right = jnp.where(col == cols - 1, 0.0, pltpu.roll(plane, cols - 1, 1))
    return (below + above) + (left + right)


def setup_kernel(
    rows,
    diff_table, uptake_table, conc_hbm, mask_hbm, layer_hbm, stiff_hbm, prod_hbm,
    s_out, g_out, r_out, gp_out, keep_out, source_out, ssum_out, part_out, ends_out,
    conc, mask, layer, stiff, prod, sems,
):
    pairs = ((mask_hbm, mask), (layer_hbm, layer), (stiff_hbm, stiff), (conc_hbm, conc), (prod_hbm, prod))
    copies = []
    for chunk in range(rows // CHUNK):
        here = pl.ds(chunk * CHUNK, CHUNK)
        copies.append([
            pltpu.make_async_copy(source.at[here], target.at[here], sems.at[k, chunk])
            for k, (source, target) in enumerate(pairs)
        ])
    for group in copies:
        for copy in group:
            copy.start()
    dtab = [diff_table[k] for k in range(LAYERS)]
    utab = [uptake_table[k] for k in range(LAYERS)]

    def plane_setup(z):
        weight = mask[z].astype(jnp.float32)
        labels = layer[z]
        s = jnp.sqrt(weight * lookup(labels, dtab) * stiff[z])
        s_out[z] = s
        keep_out[z] = 1.0 - weight * lookup(labels, utab)
        source_out[z] = weight * prod[z]
        state = conc[z]
        ssum = neighbour_sum(s)
        ssum_out[z] = ssum
        part_out[z] = state + SECTION_RATE * s * (neighbour_sum(s * state) - state * ssum)
        return s

    for z in range(rows):
        if z % CHUNK == 0:
            for copy in copies[z // CHUNK]:
                copy.wait()
        s_next = plane_setup(z)
        if z == 0:
            m = jnp.ones_like(s_next)
            gp = jnp.ones_like(s_next)
            alpha = jnp.zeros_like(s_next)
        else:
            c = RZ * s * s_next
            r = 1.0 / (m + c)
            g = c * r
            r_out[z - 1] = r
            g_out[z - 1] = g
            gp_out[z - 1] = gp
            alpha = alpha + r * gp * gp
            m = 1.0 + g * m
            gp = gp * g
        s = s_next
    gp_out[rows - 1] = gp
    ends_out[0] = m
    ends_out[1] = alpha


def halo_term(z, s_ref, state_row, s_halo, v_halo):
    return SECTION_RATE * s_ref * (v_halo - state_row * s_halo)


def forward_sweep(rows, slab, first_step, ix, nx, state_ref, s_ref, g_ref, r_ref, gp_ref, part_ref, lo_ref, hi_ref,
                  shalo_lo, shalo_hi, last_g, last_r, fwd_ref):
    row = lax.broadcasted_iota(jnp.int32, (8, lo_ref.shape[-1]), 0)
    top = jnp.where(row == 0, jnp.where(ix > 0, SECTION_RATE, 0.0), 0.0)
    bottom = jnp.where(row == 7, jnp.where(ix < nx - 1, SECTION_RATE, 0.0), 0.0)
    total = None
    prev = None
    for z in range(rows):
        st_lo, st_hi = state_ref(z, 0), state_ref(z, 1)
        s_lo, s_hi = s_ref[z, 0:8], s_ref[z, slab - 8:slab]
        sl, sh = shalo_lo[z:z + 1], shalo_hi[z:z + 1]
        vl, vh = lo_ref[z:z + 1], hi_ref[z:z + 1]
        if first_step:
            vl, vh = vl * sl, vh * sh
        extra_lo = top * s_lo * (vl - st_lo * sl)
        extra_hi = bottom * s_hi * (vh - st_hi * sh)
        part = part_ref[z]
        e = jnp.concatenate([part[0:8] + extra_lo, part[8:slab - 8], part[slab - 8:] + extra_hi], axis=0)
        if z > 0:
            e = e + g_ref[z - 1] * prev
        fwd_ref[z] = e
        r = r_ref[z] if z < rows - 1 else last_r
        term = gp_ref[z] * r * e
        total = term if z == 0 else total + term
        prev = e
    return total, last_g * prev


def first_forward_kernel(
    rows, slab, nx, nax,
    conc_ref, s_ref, g_ref, r_ref, gp_ref, part_ref, ends_ref, lo_ref, hi_ref, ax_ref,
    fwd_ref, last_ref, mine_ref, send_ref, ports_ref,
):
    ix, ia = lax.axis_index("xs"), lax.axis_index("ax")
    above = jnp.where(ia < nax - 1, RZ, 0.0)
    c = above * s_ref[rows - 1] * ax_ref[...]
    m, alpha = ends_ref[0], ends_ref[1]
    last_r = 1.0 / (m + c)
    last_g = c * last_r
    gp = gp_ref[rows - 1]
    last_ref[0] = last_g
    last_ref[1] = last_r
    a, b = forward_sweep(
        rows, slab, True, ix, nx, lambda z, side: conc_ref[z, side], s_ref, g_ref, r_ref, gp_ref, part_ref,
        lo_ref.at[1], hi_ref.at[1], lo_ref.at[0], hi_ref.at[0], last_g, last_r, fwd_ref)
    ports_ref[0] = a
    ports_ref[1] = b
    ports_ref[2] = alpha + last_r * gp * gp
    ports_ref[3] = last_g * gp
    ports_ref[4] = last_g * m
    half = slab // 2
    core = lax.rem(ia, 2)
    mine_ref[...] = ports_ref[:, pl.ds(pl.multiple_of(core * half, half), half)]
    send_ref[...] = ports_ref[:, pl.ds(pl.multiple_of((1 - core) * half, half), half)]


def second_forward_kernel(
    rows, slab, nx,
    edge_ref, s_ref, g_ref, r_ref, gp_ref, part_ref, last_ref, first_lo_ref, first_hi_ref, lo_ref, hi_ref,
    fwd_ref, mine_ref, send_ref, ports_ref,
):
    ix, ia = lax.axis_index("xs"), lax.axis_index("ax")
    a, b = forward_sweep(
        rows, slab, False, ix, nx, lambda z, side: edge_ref[side, z], s_ref, g_ref, r_ref, gp_ref, part_ref,
        lo_ref, hi_ref, first_lo_ref.at[0], first_hi_ref.at[0], last_ref[0], last_ref[1], fwd_ref)
    ports_ref[0] = a
    ports_ref[1] = b
    half = slab // 2
    core = lax.rem(ia, 2)
    mine_ref[...] = ports_ref[:, pl.ds(pl.multiple_of(core * half, half), half)]
    send_ref[...] = ports_ref[:, pl.ds(pl.multiple_of((1 - core) * half, half), half)]


def is_upper(level):
    return lax.rem(lax.div(lax.axis_index("ax"), 2 ** level), 2) == 1


def join(upper, mine, theirs):
    return jnp.where(upper, theirs, mine), jnp.where(upper, mine, theirs)


def join_coefs(level, mine, recv, lev):
    upper = is_upper(level)
    (alpha1, alpha2), (beta1, beta2), (kappa1, kappa2) = [join(upper, mine[k], recv[k]) for k in (2, 3, 4)]
    rho = 1.0 / (1.0 + kappa1 * alpha2)
    x, y = beta1 * rho, beta2 * rho
    ax, ky = alpha2 * x, kappa1 * y
    for k, value in enumerate((rho, kappa1, alpha2, beta1, beta2, x, y, ax, ky)):
        lev[k] = value
    return alpha1 + beta1 * ax, x * beta2, kappa2 + beta2 * ky


def join_rhs(level, mine, recv, lev, values):
    upper = is_upper(level)
    (a1, a2), (b1, b2) = [join(upper, mine[k], recv[k]) for k in (0, 1)]
    rho, kappa1, alpha2, beta1, beta2 = [lev[k] for k in range(5)]
    u0 = rho * (a2 + alpha2 * b1)
    q0 = rho * (b1 - kappa1 * a2)
    values[0] = u0
    values[1] = q0
    return a1 + beta1 * u0, b2 + beta2 * q0


def first_join_kernel(level, mine, recv, out, lev, values):
    out[2], out[3], out[4] = join_coefs(level, mine, recv, lev)
    out[0], out[1] = join_rhs(level, mine, recv, lev, values)


def second_join_kernel(level, mine, recv, lev, out, values):
    out[0], out[1] = join_rhs(level, mine, recv, lev, values)


def below(lev, q, top, u0, q0):
    x, y, ax, ky = [lev[k] for k in (5, 6, 7, 8)]
    return u0 + y * top + ax * q, q0 + x * q - ky * top


def descend(levels, levs, values, mine_out, send_out):
    top_level = levels - 1
    u0, q0 = values[top_level][0], values[top_level][1]
    upper = is_upper(top_level)
    q = jnp.where(upper, q0, 0.0)
    top = jnp.where(upper, 0.0, u0)
    for level in range(top_level - 1, -1, -1):
        new_top, new_q = below(levs[level], q, top, values[level][0], values[level][1])
        upper = is_upper(level)
        if level > 0:
            q, top = jnp.where(upper, new_q, q), jnp.where(upper, top, new_top)
        else:
            mine_out[0] = jnp.where(upper, new_q, q)
            mine_out[1] = jnp.where(upper, top, new_top)
            send_out[0] = jnp.where(upper, q, new_q)
            send_out[1] = jnp.where(upper, new_top, top)


def first_last_kernel(levels, *refs):
    mine, recv = refs[:2]
    levs, values = refs[2:2 + levels - 1], refs[1 + levels:2 * levels]
    mine_out, send_out, lev, last = refs[2 * levels:]
    join_coefs(levels - 1, mine, recv, lev)
    join_rhs(levels - 1, mine, recv, lev, last)
    descend(levels, list(levs) + [lev], list(values) + [last], mine_out, send_out)


def second_last_kernel(levels, *refs):
    mine, recv = refs[:2]
    levs, values = refs[2:2 + levels], refs[2 + levels:1 + 2 * levels]
    mine_out, send_out, last = refs[1 + 2 * levels:]
    join_rhs(levels - 1, mine, recv, levs[-1], last)
    descend(levels, list(levs), list(values) + [last], mine_out, send_out)


def whole_ports(own, other):
    upper = lax.rem(lax.axis_index("ax"), 2) == 1
    planes = []
    for k in (0, 1):
        low, high = jnp.where(upper, other[k], own[k]), jnp.where(upper, own[k], other[k])
        planes.append(jnp.concatenate([low, high], axis=0))
    return planes


def edge_state_kernel(
    rows, slab,
    own, other, s_ref, g_ref, r_ref, gp_ref, fwd_ref, last_ref, keep_ref, source_ref,
    edge_ref, lo_ref, hi_ref,
):
    q, top = whole_ports(own, other)
    for side in (0, 1):
        at = slice(0, 8) if side == 0 else slice(slab - 8, slab)
        u, inflow = top[at], q[at]
        for z in range(rows - 1, -1, -1):
            r = r_ref[z, at] if z < rows - 1 else last_ref[1, at]
            g = g_ref[z, at] if z < rows - 1 else last_ref[0, at]
            u = r * (fwd_ref[z, at] + gp_ref[z, at] * inflow) + g * u
            state = source_ref[z, at] + keep_ref[z, at] * u
            edge_ref[side, z] = state
            flow = s_ref[z, at] * state
            if side == 0:
                lo_ref[z:z + 1] = flow[0:1]
            else:
                hi_ref[z:z + 1] = flow[7:8]


def middle_state_kernel(
    rows, slab,
    own, other, edge_ref, s_ref, g_ref, r_ref, gp_ref, fwd_ref, last_ref, keep_ref, source_ref, ssum_ref,
    part_ref,
):
    q, top = whole_ports(own, other)
    at = slice(8, slab - 8)
    u, inflow = top[at], q[at]
    for z in range(rows - 1, -1, -1):
        r = r_ref[z, at] if z < rows - 1 else last_ref[1, at]
        g = g_ref[z, at] if z < rows - 1 else last_ref[0, at]
        u = r * (fwd_ref[z, at] + gp_ref[z, at] * inflow) + g * u
        middle = source_ref[z, at] + keep_ref[z, at] * u
        state = jnp.concatenate([edge_ref[0, z], middle, edge_ref[1, z]], axis=0)
        s = s_ref[z]
        part_ref[z] = state + SECTION_RATE * s * (neighbour_sum(s * state) - state * ssum_ref[z])


def final_kernel(
    rows, slab,
    own, other, g_ref, r_ref, gp_ref, fwd_ref, last_ref, keep_ref, source_ref,
    out_hbm, out, sems,
):
    q, u = whole_ports(own, other)
    copies = []
    for z in range(rows - 1, -1, -1):
        r = r_ref[z] if z < rows - 1 else last_ref[1]
        g = g_ref[z] if z < rows - 1 else last_ref[0]
        u = r * (fwd_ref[z] + gp_ref[z] * q) + g * u
        out[z] = source_ref[z] + keep_ref[z] * u
        if z % CHUNK == 0:
            here = pl.ds(z, CHUNK)
            copy = pltpu.make_async_copy(out.at[here], out_hbm.at[here], sems.at[z // CHUNK])
            copy.start()
            copies.append(copy)
    for copy in copies:
        copy.wait()


def edge_diffusivity(mask, layer, stiff, table):
    return jnp.sqrt(mask.astype(jnp.float32) * lookup(layer, table) * stiff)


def on_device(partners, concentration, tissue_mask, wall_layer, stiffness, production, layer_diffusivity, uptake_rate):
    rows, slab, cols = concentration.shape
    half = slab // 2
    nx, nax = lax.axis_size("xs"), lax.axis_size("ax")
    levels = len(partners)

    def call(kernel, outs, operands, scratch=(), specs=None, out_specs=None, us=1.0):
        return pl.pallas_call(
            kernel,
            out_shape=outs,
            in_specs=specs or [vspec()] * len(operands),
            out_specs=out_specs or [vspec()] * len(outs),
            scratch_shapes=list(scratch),
            compiler_params=params(),
            cost_estimate=cost(us),
        )(*operands)

    def exchange(block, level):
        return lax.ppermute(block, "ax", partners[level])

    def side(x):
        s = edge_diffusivity(tissue_mask[:, x], wall_layer[:, x], stiffness[:, x], layer_diffusivity)
        return jnp.stack([s, concentration[:, x]])

    first_s = edge_diffusivity(tissue_mask[0], wall_layer[0], stiffness[0], layer_diffusivity)
    upward = [(i, (i + 1) % nx) for i in range(nx)]
    downward = [((i + 1) % nx, i) for i in range(nx)]
    halo_lo = lax.ppermute(side(slab - 1), "xs", upward)
    halo_hi = lax.ppermute(side(0), "xs", downward)
    above_s = lax.ppermute(first_s, "ax", [((i + 1) % nax, i) for i in range(nax)])

    block = (rows, slab, cols)
    smem = pl.BlockSpec(memory_space=pltpu.SMEM)
    hbm = pl.BlockSpec(memory_space=pltpu.HBM)
    s, g, r, gp, keep, source, ssum, part, ends = call(
        functools.partial(setup_kernel, rows),
        [at_vmem(*block)] * 8 + [at_vmem(2, slab, cols)],
        [layer_diffusivity, uptake_rate, concentration, tissue_mask, wall_layer, stiffness, production],
        scratch=[
            pltpu.VMEM(block, jnp.float32), pltpu.VMEM(block, jnp.int32), pltpu.VMEM(block, jnp.int32),
            pltpu.VMEM(block, jnp.float32), pltpu.VMEM(block, jnp.float32),
            pltpu.SemaphoreType.DMA((5, rows // CHUNK)),
        ],
        specs=[smem, smem] + [hbm] * 5,
        us=5.0,
    )
    conc_edges = jnp.stack([concentration[:, :8], concentration[:, slab - 8:]], axis=1)
    fwd, last, mine, send = call(
        functools.partial(first_forward_kernel, rows, slab, nx, nax),
        [at_vmem(*block), at_vmem(2, slab, cols), at_vmem(5, half, cols), at_vmem(5, half, cols)],
        [conc_edges, s, g, r, gp, part, ends, halo_lo, halo_hi, above_s],
        scratch=[pltpu.VMEM((5, slab, cols), jnp.float32)],
    )
    levs, values = [], []
    for level in range(levels - 1):
        recv = exchange(send if level == 0 else mine, level)
        mine, lev, value = call(
            functools.partial(first_join_kernel, level),
            [at_vmem(5, half, cols), at_vmem(9, half, cols), at_vmem(2, half, cols)],
            [mine, recv],
        )
        levs.append(lev)
        values.append(value)
    recv = exchange(mine, levels - 1)
    own, send, lev = call(
        functools.partial(first_last_kernel, levels),
        [at_vmem(2, half, cols), at_vmem(2, half, cols), at_vmem(9, half, cols)],
        [mine, recv, *levs, *values],
        scratch=[pltpu.VMEM((2, half, cols), jnp.float32)],
    )
    levs.append(lev)
    other = exchange(send, 0)

    edges, lo, hi = call(
        functools.partial(edge_state_kernel, rows, slab),
        [at_vmem(2, rows, 8, cols), at_vmem(rows, cols), at_vmem(rows, cols)],
        [own, other, s, g, r, gp, fwd, last, keep, source],
    )
    from_lo = lax.ppermute(hi, "xs", upward)
    from_hi = lax.ppermute(lo, "xs", downward)
    (part,) = call(
        functools.partial(middle_state_kernel, rows, slab),
        [at_vmem(*block)],
        [own, other, edges, s, g, r, gp, fwd, last, keep, source, ssum],
        us=3.0,
    )
    fwd, mine, send = call(
        functools.partial(second_forward_kernel, rows, slab, nx),
        [at_vmem(*block), at_vmem(2, half, cols), at_vmem(2, half, cols)],
        [edges, s, g, r, gp, part, last, halo_lo, halo_hi, from_lo, from_hi],
        scratch=[pltpu.VMEM((2, slab, cols), jnp.float32)],
    )
    values = []
    for level in range(levels - 1):
        recv = exchange(send if level == 0 else mine, level)
        mine, value = call(
            functools.partial(second_join_kernel, level),
            [at_vmem(2, half, cols), at_vmem(2, half, cols)],
            [mine, recv, levs[level]],
        )
        values.append(value)
    recv = exchange(mine, levels - 1)
    own, send = call(
        functools.partial(second_last_kernel, levels),
        [at_vmem(2, half, cols), at_vmem(2, half, cols)],
        [mine, recv, *levs, *values],
        scratch=[pltpu.VMEM((2, half, cols), jnp.float32)],
    )
    other = exchange(send, 0)
    (out,) = call(
        functools.partial(final_kernel, rows, slab),
        [jax.ShapeDtypeStruct(block, jnp.float32)],
        [own, other, g, r, gp, fwd, last, keep, source],
        scratch=[pltpu.VMEM(block, jnp.float32), pltpu.SemaphoreType.DMA((rows // CHUNK,))],
        out_specs=[hbm],
    )
    return out


def join_partners():
    flips = (
        lambda y, z, c: (y, z, 1 - c),
        lambda y, z, c: (y, z ^ 1, c),
        lambda y, z, c: (y, 3 - z, c),
        lambda y, z, c: (y ^ 1, z, c),
        lambda y, z, c: (3 - y, z, c),
    )
    routes = []
    for flip in flips:
        route = []
        for i in range(32):
            y, z, c = flip(i // 8, i // 2 % 4, i % 2)
            route.append((i, y * 8 + z * 2 + c))
        routes.append(route)
    return routes


def solution(mesh):
    placed = (P("ax", "xs", None),) * 5 + (P(), P())
    return jax.shard_map(
        functools.partial(on_device, join_partners()),
        mesh=mesh, in_specs=placed, out_specs=P("ax", "xs", None), check_vma=False,
    )
```

```python
import functools

import jax
import jax.numpy as jnp
from jax import lax
from jax.experimental import pallas as pl
from jax.experimental.pallas import tpu as pltpu
from jax.sharding import PartitionSpec as P

RZ = 3072.0
SECTION_RATE = 0.05
LAYERS = 4
LIMIT = 20 * 1024 * 1024
CHUNK = 8


def at_vmem(*shape):
    return pltpu.VMEM(shape, jnp.float32)


def vspec():
    return pl.BlockSpec(memory_space=pltpu.VMEM)


def params():
    return pltpu.CompilerParams(vmem_limit_bytes=LIMIT)


def cost(us):
    return pl.CostEstimate(flops=int(us * 2e6), bytes_accessed=int(us * 3e6), transcendentals=0)


def lookup(labels, table):
    summed = jnp.where(labels == 0, table[0], 0.0)
    for layer in range(1, LAYERS):
        summed = jnp.where(labels == layer, table[layer], summed)
    return summed


def tiles_of(ref, z, slab, cols):
    return [[ref[z, t:t + 8, c:c + 128] for c in range(0, cols, 128)] for t in range(0, slab, 8)]


def neighbour_sum(tiles):
    rows, cols = len(tiles), len(tiles[0])
    row = lax.broadcasted_iota(jnp.int32, (8, 128), 0)
    lane = lax.broadcasted_iota(jnp.int32, (8, 128), 1)

    def rolled(shift, axis):
        return [[pltpu.roll(tile, shift, axis) for tile in line] for line in tiles]

    down, up, right, left = rolled(1, 0), rolled(7, 0), rolled(1, 1), rolled(127, 1)

    def at(array, t, c):
        return array[t][c] if 0 <= t < rows and 0 <= c < cols else 0.0

    return [[
        (jnp.where(row == 0, at(down, t - 1, c), down[t][c]) + jnp.where(row == 7, at(up, t + 1, c), up[t][c]))
        + (jnp.where(lane == 0, at(right, t, c - 1), right[t][c])
           + jnp.where(lane == 127, at(left, t, c + 1), left[t][c]))
        for c in range(cols)] for t in range(rows)]


def inverse(x):
    r = pl.reciprocal(x, approx=True)
    r = r * (2.0 - x * r)
    return r * (2.0 - x * r)


def edge_kernel(
    rows, slab,
    table, conc_hbm, mask_hbm, layer_hbm, stiff_hbm,
    lo_out, hi_out, first_out, conc_edges,
    mask, layer, stiff, mask_row, layer_row, stiff_row, sems,
):
    copies = []
    for side in (0, 1):
        here = pl.ds(0 if side == 0 else slab - 8, 8)
        for k, (source, target) in enumerate(
                ((mask_hbm, mask), (layer_hbm, layer), (stiff_hbm, stiff), (conc_hbm, conc_edges))):
            copies.append(pltpu.make_async_copy(source.at[:, here], target.at[side], sems.at[side, k]))
    rowcopies = []
    for k, (source, target) in enumerate(((mask_hbm, mask_row), (layer_hbm, layer_row), (stiff_hbm, stiff_row))):
        rowcopies.append(pltpu.make_async_copy(source.at[0], target, sems.at[2, k]))
    for copy in copies + rowcopies:
        copy.start()
    tab = [table[k] for k in range(LAYERS)]
    for side, out in ((0, lo_out), (1, hi_out)):
        for copy in copies[4 * side:4 * side + 4]:
            copy.wait()
        keep = slice(0, 1) if side == 0 else slice(7, 8)
        for z in range(rows):
            s = root(mask[side, z].astype(jnp.float32) * lookup(layer[side, z], tab) * stiff[side, z])
            out[0, z:z + 1] = s[keep]
            out[1, z:z + 1] = conc_edges[side, z][keep]
    for copy in rowcopies:
        copy.wait()
    first_out[...] = root(mask_row[...].astype(jnp.float32) * lookup(layer_row[...], tab) * stiff_row[...])


def root(x):
    return jnp.sqrt(x)


def setup_kernel(
    rows, slab, cols,
    table, conc_hbm, mask_hbm, layer_hbm, stiff_hbm,
    s_out, g_out, r_out, gp_out, ssum_out, part_out, ends_out,
    conc, mask, layer, stiff, sems,
):
    pairs = ((mask_hbm, mask), (layer_hbm, layer), (stiff_hbm, stiff), (conc_hbm, conc))
    copies = []
    for chunk in range(rows // CHUNK):
        here = pl.ds(chunk * CHUNK, CHUNK)
        copies.append([
            pltpu.make_async_copy(source.at[here], target.at[here], sems.at[k, chunk])
            for k, (source, target) in enumerate(pairs)
        ])
    for group in copies:
        for copy in group:
            copy.start()
    tab = [table[k] for k in range(LAYERS)]
    grid = [(t, c) for t in range(slab // 8) for c in range(cols // 128)]
    s = m = gp = alpha = None
    for z in range(rows):
        if z % CHUNK == 0:
            for copy in copies[z // CHUNK]:
                copy.wait()
        w, lab, sti, st = [tiles_of(ref, z, slab, cols) for ref in (mask, layer, stiff, conc)]
        s_next = [[root(w[t][c].astype(jnp.float32) * lookup(lab[t][c], tab) * sti[t][c])
                   for c in range(cols // 128)] for t in range(slab // 8)]
        flow = [[s_next[t][c] * st[t][c] for c in range(cols // 128)] for t in range(slab // 8)]
        ssum, vsum = neighbour_sum(s_next), neighbour_sum(flow)
        for t, c in grid:
            here = (z, pl.ds(8 * t, 8), pl.ds(128 * c, 128))
            s_out[here] = s_next[t][c]
            ssum_out[here] = ssum[t][c]
            part_out[here] = st[t][c] + SECTION_RATE * s_next[t][c] * (vsum[t][c] - st[t][c] * ssum[t][c])
        if z == 0:
            ones = {k: jnp.ones((8, 128), jnp.float32) for k in grid}
            m, gp, alpha = dict(ones), dict(ones), {k: jnp.zeros((8, 128), jnp.float32) for k in grid}
        else:
            for t, c in grid:
                k = (t, c)
                here = (z - 1, pl.ds(8 * t, 8), pl.ds(128 * c, 128))
                couple = RZ * s[t][c] * s_next[t][c]
                r = inverse(m[k] + couple)
                g = couple * r
                r_out[here] = r
                g_out[here] = g
                gp_out[here] = gp[k]
                alpha[k] = alpha[k] + r * gp[k] * gp[k]
                m[k] = 1.0 + g * m[k]
                gp[k] = gp[k] * g
        s = s_next
    for t, c in grid:
        here = (pl.ds(8 * t, 8), pl.ds(128 * c, 128))
        gp_out[(rows - 1,) + here] = gp[t, c]
        ends_out[(0,) + here] = m[t, c]
        ends_out[(1,) + here] = alpha[t, c]


def reaction_kernel(rows, uptake_table, mask_hbm, layer_hbm, prod_hbm, keep_out, source_out, mask, layer, prod, sems):
    copies = []
    for chunk in range(rows // CHUNK):
        here = pl.ds(chunk * CHUNK, CHUNK)
        copies.append([
            pltpu.make_async_copy(source.at[here], target.at[here], sems.at[k, chunk])
            for k, (source, target) in enumerate(((mask_hbm, mask), (layer_hbm, layer), (prod_hbm, prod)))
        ])
    for group in copies:
        for copy in group:
            copy.start()
    tab = [uptake_table[k] for k in range(LAYERS)]
    for z in range(rows):
        if z % CHUNK == 0:
            for copy in copies[z // CHUNK]:
                copy.wait()
        weight = mask[z].astype(jnp.float32)
        keep_out[z] = 1.0 - weight * lookup(layer[z], tab)
        source_out[z] = weight * prod[z]


def forward_sweep(rows, slab, first_step, ix, nx, state_ref, s_ref, g_ref, r_ref, gp_ref, part_ref, lo_ref, hi_ref,
                  shalo_lo, shalo_hi, last_g, last_r, fwd_ref):
    row = lax.broadcasted_iota(jnp.int32, (8, lo_ref.shape[-1]), 0)
    top = jnp.where(row == 0, jnp.where(ix > 0, SECTION_RATE, 0.0), 0.0)
    bottom = jnp.where(row == 7, jnp.where(ix < nx - 1, SECTION_RATE, 0.0), 0.0)
    total = None
    prev = None
    for z in range(rows):
        st_lo, st_hi = state_ref(z, 0), state_ref(z, 1)
        s_lo, s_hi = s_ref[z, 0:8], s_ref[z, slab - 8:slab]
        sl, sh = shalo_lo[z:z + 1], shalo_hi[z:z + 1]
        vl, vh = lo_ref[z:z + 1], hi_ref[z:z + 1]
        if first_step:
            vl, vh = vl * sl, vh * sh
        extra_lo = top * s_lo * (vl - st_lo * sl)
        extra_hi = bottom * s_hi * (vh - st_hi * sh)
        part = part_ref[z]
        e = jnp.concatenate([part[0:8] + extra_lo, part[8:slab - 8], part[slab - 8:] + extra_hi], axis=0)
        if z > 0:
            e = e + g_ref[z - 1] * prev
        fwd_ref[z] = e
        r = r_ref[z] if z < rows - 1 else last_r
        term = gp_ref[z] * r * e
        total = term if z == 0 else total + term
        prev = e
    return total, last_g * prev


def first_forward_kernel(
    rows, slab, nx, nax,
    conc_ref, s_ref, g_ref, r_ref, gp_ref, part_ref, ends_ref, lo_ref, hi_ref, ax_ref,
    fwd_ref, last_ref, mine_ref, send_ref, ports_ref,
):
    ix, ia = lax.axis_index("xs"), lax.axis_index("ax")
    above = jnp.where(ia < nax - 1, RZ, 0.0)
    c = above * s_ref[rows - 1] * ax_ref[...]
    m, alpha = ends_ref[0], ends_ref[1]
    last_r = 1.0 / (m + c)
    last_g = c * last_r
    gp = gp_ref[rows - 1]
    last_ref[0] = last_g
    last_ref[1] = last_r
    a, b = forward_sweep(
        rows, slab, True, ix, nx, lambda z, side: conc_ref[side, z], s_ref, g_ref, r_ref, gp_ref, part_ref,
        lo_ref.at[1], hi_ref.at[1], lo_ref.at[0], hi_ref.at[0], last_g, last_r, fwd_ref)
    ports_ref[0] = a
    ports_ref[1] = b
    ports_ref[2] = alpha + last_r * gp * gp
    ports_ref[3] = last_g * gp
    ports_ref[4] = last_g * m
    split_ports(slab, ports_ref, mine_ref, send_ref)


def second_forward_kernel(
    rows, slab, nx,
    edge_ref, s_ref, g_ref, r_ref, gp_ref, part_ref, last_ref, first_lo_ref, first_hi_ref, lo_ref, hi_ref,
    fwd_ref, mine_ref, send_ref, ports_ref,
):
    ix, ia = lax.axis_index("xs"), lax.axis_index("ax")
    a, b = forward_sweep(
        rows, slab, False, ix, nx, lambda z, side: edge_ref[side, z], s_ref, g_ref, r_ref, gp_ref, part_ref,
        lo_ref, hi_ref, first_lo_ref.at[0], first_hi_ref.at[0], last_ref[0], last_ref[1], fwd_ref)
    ports_ref[0] = a
    ports_ref[1] = b
    split_ports(slab, ports_ref, mine_ref, send_ref)


def place():
    i = lax.axis_index("ax")
    core, z, y = lax.rem(i, 2), lax.rem(lax.div(i, 2), 4), lax.div(i, 8)
    return core, z, y, lax.rem(core + z + y, 2)


def split_ports(slab, ports_ref, mine_ref, send_ref):
    half = slab // 2
    own = place()[3]
    mine_ref[...] = ports_ref[:, pl.ds(pl.multiple_of(own * half, half), half)]
    send_ref[...] = ports_ref[:, pl.ds(pl.multiple_of((1 - own) * half, half), half)]


def pick(index, options):
    value = options[0]
    for k in range(1, len(options)):
        value = jnp.where(index == k, options[k], value)
    return value


def ordered(index, mine, received):
    return [pick(index ^ j, [mine] + received) for j in range(1 + len(received))]


JOIN_COEFS = 9


def join_coefs(low, high, lev, at):
    (alpha1, beta1, kappa1), (alpha2, beta2, kappa2) = low, high
    rho = inverse(1.0 + kappa1 * alpha2)
    x, y = beta1 * rho, beta2 * rho
    ax, ky = alpha2 * x, kappa1 * y
    for k, value in enumerate((rho, kappa1, alpha2, beta1, beta2, x, y, ax, ky)):
        lev[at * JOIN_COEFS + k] = value
    return alpha1 + beta1 * ax, x * beta2, kappa2 + beta2 * ky


def join_rhs(low, high, lev, at, values):
    (a1, b1), (a2, b2) = low, high
    rho, kappa1, alpha2, beta1, beta2 = [lev[at * JOIN_COEFS + k] for k in range(5)]
    u0 = rho * (a2 + alpha2 * b1)
    q0 = rho * (b1 - kappa1 * a2)
    values[2 * at] = u0
    values[2 * at + 1] = q0
    return a1 + beta1 * u0, b2 + beta2 * q0


def join_all(groups, join):
    if len(groups) == 2:
        return join(groups[0], groups[1], 0)
    return join(join(groups[0], groups[1], 0), join(groups[2], groups[3], 1), 2)


def stage_coefs(index, mine, received, lev):
    planes = [ordered(index, mine[k], [r[k] for r in received]) for k in (2, 3, 4)]
    return join_all(list(zip(*planes)), lambda low, high, at: join_coefs(low, high, lev, at))


def stage_rhs(index, mine, received, lev, values):
    planes = [ordered(index, mine[k], [r[k] for r in received]) for k in (0, 1)]
    return join_all(list(zip(*planes)), lambda low, high, at: join_rhs(low, high, lev, at, values))


def stage_index(stage):
    return place()[stage]


def first_join_kernel(stage, count, mine, *refs):
    received, (out, lev, values) = refs[:count], refs[count:]
    index = stage_index(stage)
    out[2], out[3], out[4] = stage_coefs(index, mine, received, lev)
    out[0], out[1] = stage_rhs(index, mine, received, lev, values)


def second_join_kernel(stage, count, mine, *refs):
    received, (lev, out, values) = refs[:count], refs[count:]
    out[0], out[1] = stage_rhs(stage_index(stage), mine, received, lev, values)


def inside(lev, values, at, q, top):
    x, y, ax, ky = [pick(at[0], [lev[j * JOIN_COEFS + k] for j in at[1]]) for k in (5, 6, 7, 8)]
    u0, q0 = [pick(at[0], [values[2 * j + k] for j in at[1]]) for k in (0, 1)]
    if q is None:
        return u0, q0
    return u0 + y * top + ax * q, q0 + x * q - ky * top


def descend(levs, values, mine_out, send_out):
    core, z, y, _ = place()
    q = top = None
    for stage, index in ((2, y), (1, z)):
        lev, value = levs[stage], values[stage]
        mid_top, mid_q = inside(lev, value, (0, (2,)), q, top)
        if q is None:
            q = top = jnp.zeros_like(mid_q)
        high = index >= 2
        q, top = jnp.where(high, mid_q, q), jnp.where(high, top, mid_top)
        mid_top, mid_q = inside(lev, value, (lax.div(index, 2), (0, 1)), q, top)
        odd = lax.rem(index, 2) == 1
        q, top = jnp.where(odd, mid_q, q), jnp.where(odd, top, mid_top)
    mid_top, mid_q = inside(levs[0], values[0], (0, (0,)), q, top)
    upper = core == 1
    mine_out[0], mine_out[1] = jnp.where(upper, mid_q, q), jnp.where(upper, top, mid_top)
    send_out[0], send_out[1] = jnp.where(upper, q, mid_q), jnp.where(upper, mid_top, top)


def first_last_kernel(count, mine, *refs):
    received = refs[:count]
    lev0, lev1, val0, val1, mine_out, send_out, lev2, val2 = refs[count:]
    index = stage_index(2)
    stage_coefs(index, mine, received, lev2)
    stage_rhs(index, mine, received, lev2, val2)
    descend((lev0, lev1, lev2), (val0, val1, val2), mine_out, send_out)


def second_last_kernel(count, mine, *refs):
    received = refs[:count]
    lev0, lev1, lev2, val0, val1, mine_out, send_out, val2 = refs[count:]
    stage_rhs(stage_index(2), mine, received, lev2, val2)
    descend((lev0, lev1, lev2), (val0, val1, val2), mine_out, send_out)


def whole_ports(own, other):
    second = place()[3] == 1
    planes = []
    for k in (0, 1):
        low, high = jnp.where(second, other[k], own[k]), jnp.where(second, own[k], other[k])
        planes.append(jnp.concatenate([low, high], axis=0))
    return planes


def edge_state_kernel(
    rows, slab,
    own, other, s_ref, g_ref, r_ref, gp_ref, fwd_ref, last_ref, keep_ref, source_ref,
    edge_ref, lo_ref, hi_ref,
):
    q, top = whole_ports(own, other)
    for side in (0, 1):
        at = slice(0, 8) if side == 0 else slice(slab - 8, slab)
        u, inflow = top[at], q[at]
        for z in range(rows - 1, -1, -1):
            r = r_ref[z, at] if z < rows - 1 else last_ref[1, at]
            g = g_ref[z, at] if z < rows - 1 else last_ref[0, at]
            u = r * (fwd_ref[z, at] + gp_ref[z, at] * inflow) + g * u
            state = source_ref[z, at] + keep_ref[z, at] * u
            edge_ref[side, z] = state
            flow = s_ref[z, at] * state
            if side == 0:
                lo_ref[z:z + 1] = flow[0:1]
            else:
                hi_ref[z:z + 1] = flow[7:8]


def middle_state_kernel(
    rows, slab, cols,
    own, other, edge_ref, s_ref, g_ref, r_ref, gp_ref, fwd_ref, last_ref, keep_ref, source_ref, ssum_ref,
    part_ref,
):
    q, top = whole_ports(own, other)
    at = slice(8, slab - 8)
    u, inflow = top[at], q[at]
    for z in range(rows - 1, -1, -1):
        r = r_ref[z, at] if z < rows - 1 else last_ref[1, at]
        g = g_ref[z, at] if z < rows - 1 else last_ref[0, at]
        u = r * (fwd_ref[z, at] + gp_ref[z, at] * inflow) + g * u
        middle = source_ref[z, at] + keep_ref[z, at] * u
        planes = [edge_ref[0, z]] + [middle[t:t + 8] for t in range(0, slab - 16, 8)] + [edge_ref[1, z]]
        state = [[plane[:, c:c + 128] for c in range(0, cols, 128)] for plane in planes]
        s, ssum = tiles_of(s_ref, z, slab, cols), tiles_of(ssum_ref, z, slab, cols)
        vsum = neighbour_sum([[x * y for x, y in zip(*lines)] for lines in zip(s, state)])
        for t in range(slab // 8):
            for c in range(cols // 128):
                part_ref[z, 8 * t:8 * t + 8, 128 * c:128 * c + 128] = state[t][c] + SECTION_RATE * s[t][c] * (
                    vsum[t][c] - state[t][c] * ssum[t][c])


def final_kernel(
    rows, slab,
    own, other, g_ref, r_ref, gp_ref, fwd_ref, last_ref, keep_ref, source_ref,
    out_hbm, out, sems,
):
    q, u = whole_ports(own, other)
    copies = []
    for z in range(rows - 1, -1, -1):
        r = r_ref[z] if z < rows - 1 else last_ref[1]
        g = g_ref[z] if z < rows - 1 else last_ref[0]
        u = r * (fwd_ref[z] + gp_ref[z] * q) + g * u
        out[z] = source_ref[z] + keep_ref[z] * u
        if z % CHUNK == 0:
            here = pl.ds(z, CHUNK)
            copy = pltpu.make_async_copy(out.at[here], out_hbm.at[here], sems.at[z // CHUNK])
            copy.start()
            copies.append(copy)
    for copy in copies:
        copy.wait()


def on_device(partners, concentration, tissue_mask, wall_layer, stiffness, production, layer_diffusivity, uptake_rate):
    rows, slab, cols = concentration.shape
    half = slab // 2
    nx, nax = lax.axis_size("xs"), lax.axis_size("ax")
    block, edge = (rows, slab, cols), (2, rows, 8, cols)
    smem = pl.BlockSpec(memory_space=pltpu.SMEM)
    hbm = pl.BlockSpec(memory_space=pltpu.HBM)

    def in_hbm(x):
        return pltpu.with_memory_space_constraint(x, pltpu.HBM)

    def call(kernel, outs, operands, scratch=(), specs=None, out_specs=None, us=1.0):
        return pl.pallas_call(
            kernel,
            out_shape=outs,
            in_specs=specs or [vspec()] * len(operands),
            out_specs=out_specs or [vspec()] * len(outs),
            scratch_shapes=list(scratch),
            compiler_params=params(),
            cost_estimate=cost(us),
        )(*operands)

    def exchange(block, stage):
        return [lax.ppermute(block, "ax", route) for route in partners[stage]]

    def f32(*shape):
        return pltpu.VMEM(shape, jnp.float32)

    def i32(*shape):
        return pltpu.VMEM(shape, jnp.int32)

    conc, mask, layer, stiff, prod = [
        in_hbm(x) for x in (concentration, tissue_mask, wall_layer, stiffness, production)]
    lo, hi, first_s, conc_edges = call(
        functools.partial(edge_kernel, rows, slab),
        [at_vmem(2, rows, cols), at_vmem(2, rows, cols), at_vmem(slab, cols), at_vmem(*edge)],
        [layer_diffusivity, conc, mask, layer, stiff],
        scratch=[i32(*edge), i32(*edge), f32(*edge), i32(slab, cols), i32(slab, cols), f32(slab, cols),
                 pltpu.SemaphoreType.DMA((3, 4))],
        specs=[smem] + [hbm] * 4,
    )
    upward = [(i, (i + 1) % nx) for i in range(nx)]
    downward = [((i + 1) % nx, i) for i in range(nx)]
    halo_lo = lax.ppermute(hi, "xs", upward)
    halo_hi = lax.ppermute(lo, "xs", downward)
    above_s = lax.ppermute(first_s, "ax", [((i + 1) % nax, i) for i in range(nax)])

    s, g, r, gp, ssum, part, ends = call(
        functools.partial(setup_kernel, rows, slab, cols),
        [at_vmem(*block)] * 6 + [at_vmem(2, slab, cols)],
        [layer_diffusivity, conc, mask, layer, stiff],
        scratch=[f32(*block), i32(*block), i32(*block), f32(*block), pltpu.SemaphoreType.DMA((4, rows // CHUNK))],
        specs=[smem] + [hbm] * 4,
        us=5.0,
    )
    fwd, last, mine, send = call(
        functools.partial(first_forward_kernel, rows, slab, nx, nax),
        [at_vmem(*block), at_vmem(2, slab, cols), at_vmem(5, half, cols), at_vmem(5, half, cols)],
        [conc_edges, s, g, r, gp, part, ends, halo_lo, halo_hi, above_s],
        scratch=[f32(5, slab, cols)],
    )

    levs, values = [], []
    for stage in (0, 1):
        received = exchange(mine if stage else send, stage)
        joins = len(received)
        if stage == 1:
            uptake_late, mine = lax.optimization_barrier((uptake_rate, mine))
            keep, source = call(
                functools.partial(reaction_kernel, rows),
                [at_vmem(*block)] * 2,
                [uptake_late, mask, layer, prod],
                scratch=[i32(*block), i32(*block), f32(*block), pltpu.SemaphoreType.DMA((3, rows // CHUNK))],
                specs=[smem] + [hbm] * 3,
                us=2.0,
            )
            mine, keep, source = lax.optimization_barrier((mine, keep, source))
        mine, lev, value = call(
            functools.partial(first_join_kernel, stage, joins),
            [at_vmem(5, half, cols), at_vmem(JOIN_COEFS * joins, half, cols), at_vmem(2 * joins, half, cols)],
            [mine, *received],
        )
        levs.append(lev)
        values.append(value)
    received = exchange(mine, 2)
    joins = len(received)
    own, send, lev = call(
        functools.partial(first_last_kernel, joins),
        [at_vmem(2, half, cols), at_vmem(2, half, cols), at_vmem(JOIN_COEFS * joins, half, cols)],
        [mine, *received, *levs, *values],
        scratch=[f32(2 * joins, half, cols)],
    )
    levs.append(lev)
    (other,) = exchange(send, 0)

    edges, lo, hi = call(
        functools.partial(edge_state_kernel, rows, slab),
        [at_vmem(*edge), at_vmem(rows, cols), at_vmem(rows, cols)],
        [own, other, s, g, r, gp, fwd, last, keep, source],
    )
    from_lo = lax.ppermute(hi, "xs", upward)
    from_hi = lax.ppermute(lo, "xs", downward)
    (part,) = call(
        functools.partial(middle_state_kernel, rows, slab, cols),
        [at_vmem(*block)],
        [own, other, edges, s, g, r, gp, fwd, last, keep, source, ssum],
        us=3.0,
    )
    fwd, mine, send = call(
        functools.partial(second_forward_kernel, rows, slab, nx),
        [at_vmem(*block), at_vmem(2, half, cols), at_vmem(2, half, cols)],
        [edges, s, g, r, gp, part, last, halo_lo, halo_hi, from_lo, from_hi],
        scratch=[f32(2, slab, cols)],
    )
    values = []
    for stage in (0, 1):
        received = exchange(mine if stage else send, stage)
        joins = len(received)
        mine, value = call(
            functools.partial(second_join_kernel, stage, joins),
            [at_vmem(2, half, cols), at_vmem(2 * joins, half, cols)],
            [mine, *received, levs[stage]],
        )
        values.append(value)
    received = exchange(mine, 2)
    joins = len(received)
    own, send = call(
        functools.partial(second_last_kernel, joins),
        [at_vmem(2, half, cols), at_vmem(2, half, cols)],
        [mine, *received, *levs, *values],
        scratch=[f32(2 * joins, half, cols)],
    )
    (other,) = exchange(send, 0)
    (out,) = call(
        functools.partial(final_kernel, rows, slab),
        [jax.ShapeDtypeStruct(block, jnp.float32)],
        [own, other, g, r, gp, fwd, last, keep, source],
        scratch=[f32(*block), pltpu.SemaphoreType.DMA((rows // CHUNK,))],
        out_specs=[hbm],
    )
    return out


def join_partners():
    stages = (
        (lambda y, z, c: (y, z, 1 - c),),
        tuple(lambda y, z, c, k=k: (y, z ^ k, c ^ (k & 1)) for k in (1, 2, 3)),
        tuple(lambda y, z, c, k=k: (y ^ k, z, c ^ (k & 1)) for k in (1, 2, 3)),
    )
    routes = []
    for flips in stages:
        routes.append([])
        for flip in flips:
            route = []
            for i in range(32):
                y, z, c = flip(i // 8, i // 2 % 4, i % 2)
                route.append((i, y * 8 + z * 2 + c))
            routes[-1].append(route)
    return routes


def solution(mesh):
    placed = (P("ax", "xs", None),) * 5 + (P(), P())
    return jax.shard_map(
        functools.partial(on_device, join_partners()),
        mesh=mesh, in_specs=placed, out_specs=P("ax", "xs", None), check_vma=False,
    )
```

```python
import functools

import jax
import jax.numpy as jnp
from jax import lax
from jax.experimental import pallas as pl
from jax.experimental.pallas import tpu as pltpu
from jax.sharding import PartitionSpec as P

RZ = 3072.0
SECTION_RATE = 0.05
LAYERS = 4
LIMIT = 24 * 1024 * 1024
CHUNK = 8
PLANES = 5
JOIN_COEFS = 9
ORDER = (1, 2, 3)


def at_vmem(*shape):
    return pltpu.VMEM(shape, jnp.float32)


def vspec():
    return pl.BlockSpec(memory_space=pltpu.VMEM)


def params():
    return pltpu.CompilerParams(vmem_limit_bytes=LIMIT)


def cost(us):
    return pl.CostEstimate(flops=int(us * 2e6), bytes_accessed=int(us * 3e6), transcendentals=0)


def lookup(labels, table):
    value = table[LAYERS - 1]
    for layer in range(LAYERS - 1):
        value = jnp.where(labels == layer, table[layer], value)
    return value


def root_diffusivity(mask, layer, stiff, table):
    inside = lookup(layer, table) * stiff
    return jnp.where(mask == 0, 0.0, inside * lax.rsqrt(inside))


def inverse(x):
    return pl.reciprocal(x, approx=True)


def tiles_of(ref, z, slab, cols):
    return [[ref[z, t:t + 8, c:c + 128] for c in range(0, cols, 128)] for t in range(0, slab, 8)]


def neighbour_sum(tiles, border=None):
    rows, cols = len(tiles), len(tiles[0])
    row = lax.broadcasted_iota(jnp.int32, (8, 128), 0)
    lane = lax.broadcasted_iota(jnp.int32, (8, 128), 1)

    def rolled(shift, axis):
        return [[pltpu.roll(tile, shift, axis) for tile in line] for line in tiles]

    down, up, right, left = rolled(1, 0), rolled(7, 0), rolled(1, 1), rolled(127, 1)
    if border is not None:
        down.append([pltpu.roll(tile, 1, 0) for tile in border])
        up.append([pltpu.roll(tile, 7, 0) for tile in border])

    def at(array, t, c):
        if 0 <= c < cols and 0 <= t < rows:
            return array[t][c]
        return 0.0 if border is None or not 0 <= c < cols else array[rows][c]

    return [[
        (jnp.where(row == 0, at(down, t - 1, c), down[t][c]) + jnp.where(row == 7, at(up, t + 1, c), up[t][c]))
        + (jnp.where(lane == 0, at(right, t, c - 1), right[t][c])
           + jnp.where(lane == 127, at(left, t, c + 1), left[t][c]))
        for c in range(cols)] for t in range(rows)]


def along_cols(plane):
    cols = plane.shape[-1]
    lane = lax.broadcasted_iota(jnp.int32, plane.shape, 1)
    return (jnp.where(lane == 0, 0.0, pltpu.roll(plane, 1, 1))
            + jnp.where(lane == cols - 1, 0.0, pltpu.roll(plane, cols - 1, 1)))


def read_table(table):
    return [table[k] for k in range(LAYERS)]


def edge_kernel(
    slab, cols,
    diff_table, uptake_table, conc_hbm, mask_hbm, layer_hbm, stiff_hbm, prod_hbm,
    lo_out, hi_out, first_out,
    mask, layer, floats, mask_row, layer_row, stiff_row, sems, row_sems,
):
    copies = []
    for side in (0, 1):
        sources = []
        for depth in (0, 1):
            x = depth if side == 0 else slab - 1 - depth
            sources += [(mask_hbm.at[:, x], mask.at[side, depth]), (layer_hbm.at[:, x], layer.at[side, depth]),
                        (stiff_hbm.at[:, x], floats.at[side, depth]), (conc_hbm.at[:, x], floats.at[side, 2 + depth])]
        sources.append((prod_hbm.at[:, 0 if side == 0 else slab - 1], floats.at[side, 4]))
        copies.append([
            pltpu.make_async_copy(source, target, sems.at[side, k]) for k, (source, target) in enumerate(sources)])
    copies.append([
        pltpu.make_async_copy(source.at[0], target, row_sems.at[k])
        for k, (source, target) in enumerate(((mask_hbm, mask_row), (layer_hbm, layer_row), (stiff_hbm, stiff_row)))])
    for group in copies:
        for copy in group:
            copy.start()
    table, uptakes = read_table(diff_table), read_table(uptake_table)
    for side, out in ((0, lo_out), (1, hi_out)):
        for copy in copies[side]:
            copy.wait()
        s, inner = [root_diffusivity(mask[side, d], layer[side, d], floats[side, d], table) for d in (0, 1)]
        state = floats[side, 2]
        ssum = inner + along_cols(s)
        vsum = inner * floats[side, 3] + along_cols(s * state)
        weight = mask[side, 0].astype(jnp.float32)
        out[0] = s
        out[1] = state
        out[2] = state + SECTION_RATE * s * (vsum - state * ssum)
        out[3] = 1.0 - weight * lookup(layer[side, 0], uptakes)
        out[4] = weight * floats[side, 4]
    for copy in copies[2]:
        copy.wait()
    first_out[...] = root_diffusivity(mask_row[...], layer_row[...], stiff_row[...], table)


def setup_kernel(
    rows, slab, cols,
    table, conc_hbm, mask_hbm, layer_hbm, stiff_hbm,
    s_out, g_out, r_out, gp_out, ssum_out, part_out, ends_out,
    conc, mask, layer, stiff, sems,
):
    pairs = ((mask_hbm, mask), (layer_hbm, layer), (stiff_hbm, stiff), (conc_hbm, conc))
    copies = []
    for chunk in range(rows // CHUNK):
        here = pl.ds(chunk * CHUNK, CHUNK)
        copies.append([
            pltpu.make_async_copy(source.at[here], target.at[here], sems.at[k, chunk])
            for k, (source, target) in enumerate(pairs)
        ])
    for group in copies:
        for copy in group:
            copy.start()
    weights = read_table(table)
    grid = [(t, c) for t in range(slab // 8) for c in range(cols // 128)]
    s = m = gp = alpha = None
    for z in range(rows):
        if z % CHUNK == 0:
            for copy in copies[z // CHUNK]:
                copy.wait()
        w, lab, sti, st = [tiles_of(ref, z, slab, cols) for ref in (mask, layer, stiff, conc)]
        s_next = [[root_diffusivity(w[t][c], lab[t][c], sti[t][c], weights)
                   for c in range(cols // 128)] for t in range(slab // 8)]
        flow = [[s_next[t][c] * st[t][c] for c in range(cols // 128)] for t in range(slab // 8)]
        ssum, vsum = neighbour_sum(s_next), neighbour_sum(flow)
        for t, c in grid:
            here = (z, pl.ds(8 * t, 8), pl.ds(128 * c, 128))
            s_out[here] = s_next[t][c]
            ssum_out[here] = ssum[t][c]
            part_out[here] = st[t][c] + SECTION_RATE * s_next[t][c] * (vsum[t][c] - st[t][c] * ssum[t][c])
        if z == 0:
            ones = {k: jnp.ones((8, 128), jnp.float32) for k in grid}
            m, gp, alpha = dict(ones), dict(ones), {k: jnp.zeros((8, 128), jnp.float32) for k in grid}
        else:
            for t, c in grid:
                k = (t, c)
                here = (z - 1, pl.ds(8 * t, 8), pl.ds(128 * c, 128))
                couple = RZ * s[t][c] * s_next[t][c]
                r = inverse(m[k] + couple)
                g = couple * r
                r_out[here] = r
                g_out[here] = g
                gp_out[here] = gp[k]
                alpha[k] = alpha[k] + r * (gp[k] * gp[k])
                m[k] = 1.0 + g * m[k]
                gp[k] = gp[k] * g
        s = s_next
    for t, c in grid:
        here = (pl.ds(8 * t, 8), pl.ds(128 * c, 128))
        gp_out[(rows - 1,) + here] = gp[t, c]
        ends_out[(0,) + here] = m[t, c]
        ends_out[(1,) + here] = alpha[t, c]


def reaction_kernel(rows, uptake_table, mask_hbm, layer_hbm, prod_hbm, keep_out, source_out, mask, layer, prod, sems):
    copies = []
    for chunk in range(rows // CHUNK):
        here = pl.ds(chunk * CHUNK, CHUNK)
        copies.append([
            pltpu.make_async_copy(source.at[here], target.at[here], sems.at[k, chunk])
            for k, (source, target) in enumerate(((mask_hbm, mask), (layer_hbm, layer), (prod_hbm, prod)))
        ])
    for group in copies:
        for copy in group:
            copy.start()
    tab = read_table(uptake_table)
    for z in range(rows):
        if z % CHUNK == 0:
            for copy in copies[z // CHUNK]:
                copy.wait()
        weight = mask[z].astype(jnp.float32)
        keep_out[z] = 1.0 - weight * lookup(layer[z], tab)
        source_out[z] = weight * prod[z]


def tile_of(tiles, k):
    return tiles[8 * k:8 * k + 8]


def first_forward_kernel(
    rows, slab, cols, nx, nax,
    own_lo, own_hi, s_ref, g_ref, r_ref, gp_ref, part_ref, ends_ref, from_lo, from_hi, above_ref,
    fwd_ref, last_ref, mine_ref, send_ref, border_ref,
    ports_ref, border_ports, lines,
):
    ix, ia = lax.axis_index("xs"), lax.axis_index("ax")
    above = jnp.where(ia < nax - 1, RZ, 0.0)
    c = above * s_ref[rows - 1] * above_ref[...]
    m, alpha = ends_ref[0], ends_ref[1]
    last_r = inverse(m + c)
    last_g = c * last_r
    gp = gp_ref[rows - 1]
    last_ref[0] = last_g
    last_ref[1] = last_r
    ports_ref[2] = alpha + last_r * gp * gp
    ports_ref[3] = last_g * gp
    ports_ref[4] = last_g * m

    for side, (own, halo, exists) in enumerate(((own_lo, from_lo, ix > 0), (own_hi, from_hi, ix < nx - 1))):
        s_own, state_own = own[0], own[1]
        s = jnp.where(exists, halo[0], 0.0)
        state = halo[1]
        flux = SECTION_RATE * s_own * s * (state - state_own)
        lines[side, 0] = s
        lines[side, 1] = halo[2] - flux
        lines[side, 2] = RZ * s * pltpu.roll(s, rows - 1, 0)
        lines[side, 3] = flux
        lines[side, 4] = halo[3]
        lines[side, 5] = halo[4]

    row = lax.broadcasted_iota(jnp.int32, (8, cols), 0)
    is_lo = row == 7

    def border(k, z):
        return jnp.where(is_lo, lines[0, k, z:z + 1], lines[1, k, z:z + 1])

    total = prev = None
    for z in range(rows):
        part = part_ref[z]
        edges = (jnp.where(row == 0, lines[0, 3, z:z + 1], 0.0), jnp.where(row == 7, lines[1, 3, z:z + 1], 0.0))
        e = jnp.concatenate([part[0:8] + edges[0], part[8:slab - 8], part[slab - 8:] + edges[1]], axis=0)
        if z > 0:
            e = e + g_ref[z - 1] * prev
        fwd_ref[z] = e
        term = gp_ref[z] * (r_ref[z] if z < rows - 1 else last_r) * e
        total = term if z == 0 else total + term
        prev = e

        sb, eb = border(0, z), border(1, z)
        if z == 0:
            mb = gpb = jnp.ones_like(sb)
            first = sb
        else:
            eb = eb + gb * fb
            mb = 1.0 + gb * mb
            gpb = gpb * gb
        if z < rows - 1:
            cb = border(2, z)
            rb = inverse(mb + cb)
            gb = cb * rb
        else:
            rb = inverse(mb)
            gb = jnp.zeros_like(rb)
        fb = eb
        grb = gpb * rb
        ab = grb * gpb if z == 0 else ab + grb * gpb
        pb = grb * eb if z == 0 else pb + grb * eb
        for k, value in enumerate((sb, gb, rb, gpb, fb, border(4, z), border(5, z))):
            border_ref[k, z] = value
    ports_ref[0] = total
    ports_ref[1] = last_g * prev
    zero = jnp.zeros_like(sb)
    for k, value in enumerate((ab, grb, rb, pb, rb * fb, first, sb, zero)):
        border_ports[0, k:k + 1] = value[7:8]
        border_ports[1, k:k + 1] = value[0:1]
    half = place()[3]
    for out, which in ((mine_ref, half), (send_ref, 1 - half)):
        split_ports(slab, PLANES, ports_ref, out, which)
        out[2 * PLANES] = border_ports[which]


def split_ports(slab, planes, ports_ref, out, which):
    for t in range(slab // 16):
        at = pl.ds(pl.multiple_of(which * (slab // 2) + 8 * t, 8), 8)
        for k in range(planes):
            out[2 * k + t] = ports_ref[k, at]


def place():
    i = lax.axis_index("ax")
    core, z, y = lax.rem(i, 2), lax.rem(lax.div(i, 2), 4), lax.div(i, 8)
    return core, z, y, lax.rem(core + z + y, 2)


def pick(index, options):
    value = options[0]
    for k in range(1, len(options)):
        value = jnp.where(index == k, options[k], value)
    return value


def ordered(index, mine, received):
    return [pick(index ^ j, [mine] + received) for j in range(1 + len(received))]


def main_planes(stack, planes):
    return [stack[2 * k:2 * k + 2] for k in planes]


def put(stack, at, value):
    stack[2 * at:2 * at + 2] = value


def join_coefs(low, high, lev, at):
    (alpha1, beta1, kappa1), (alpha2, beta2, kappa2) = low, high
    rho = inverse(1.0 + kappa1 * alpha2)
    x, y = beta1 * rho, beta2 * rho
    ax, ky = alpha2 * x, kappa1 * y
    for k, value in enumerate((rho, kappa1, alpha2, beta1, beta2, x, y, ax, ky)):
        put(lev, at * JOIN_COEFS + k, value)
    return alpha1 + beta1 * ax, x * beta2, kappa2 + beta2 * ky


def join_rhs(low, high, lev, at, values):
    (a1, b1), (a2, b2) = low, high
    rho, kappa1, alpha2, beta1, beta2 = main_planes(lev, range(at * JOIN_COEFS, at * JOIN_COEFS + 5))
    u0 = rho * (a2 + alpha2 * b1)
    q0 = rho * (b1 - kappa1 * a2)
    put(values, 2 * at, u0)
    put(values, 2 * at + 1, q0)
    return a1 + beta1 * u0, b2 + beta2 * q0


def join_border(low, high, lev, at):
    (a1, b1, d1, first1, last1, s_first, s1), (a2, b2, d2, first2, last2, s2, s_last) = low, high
    c = RZ * s1 * s2
    k = c * inverse(1.0 + c * (a2 + d1))
    f, k1, k2 = k * (first2 - last1), k * b1, k * b2
    for j, value in enumerate((f, k1, k2)):
        lev[at, j:j + 1] = value
    return a1 - k1 * b1, k1 * b2, d2 - k2 * b2, first1 + b1 * f, last2 - b2 * f, s_first, s_last


def join_all(groups, join):
    if len(groups) == 2:
        return join(groups[0], groups[1], 0)
    return join(join(groups[0], groups[1], 0), join(groups[2], groups[3], 1), 2)


def stage_coefs(index, mine, received, lev):
    stacks = [main_planes(stack, (2, 3, 4)) for stack in (mine, *received)]
    planes = [ordered(index, own[0], list(own[1:])) for own in zip(*stacks)]
    return join_all(list(zip(*planes)), lambda low, high, at: join_coefs(low, high, lev, at))


def stage_rhs(index, mine, received, lev, values):
    stacks = [main_planes(stack, (0, 1)) for stack in (mine, *received)]
    planes = [ordered(index, own[0], list(own[1:])) for own in zip(*stacks)]
    return join_all(list(zip(*planes)), lambda low, high, at: join_rhs(low, high, lev, at, values))


def stage_border(index, mine, received, lev):
    tiles = ordered(index, mine[2 * PLANES], [stack[2 * PLANES] for stack in received])
    groups = [[tile[k:k + 1] for k in range(7)] for tile in tiles]
    return join_all(groups, lambda low, high, at: join_border(low, high, lev, at))


def stage_index(stage):
    return place()[stage]


def first_join_kernel(stage, count, mine, *refs):
    received, (out, lev, values, border_lev) = refs[:count], refs[count:]
    index = stage_index(stage)
    for k, value in zip((2, 3, 4), stage_coefs(index, mine, received, lev)):
        put(out, k, value)
    for k, value in zip((0, 1), stage_rhs(index, mine, received, lev, values)):
        put(out, k, value)
    for k, value in enumerate(stage_border(index, mine, received, border_lev)):
        out[2 * PLANES, k:k + 1] = value
    out[2 * PLANES, 7:8] = jnp.zeros_like(value)


def second_join_kernel(stage, count, mine, *refs):
    received, (lev, out, values) = refs[:count], refs[count:]
    for k, value in zip((0, 1), stage_rhs(stage_index(stage), mine, received, lev, values)):
        put(out, k, value)


def choose(which, ats, stack, width, k):
    return pick(which, [stack[2 * (j * width + k):2 * (j * width + k) + 2] for j in ats])


def inside(lev, values, which, ats, q, top):
    u0, q0 = [choose(which, ats, values, 2, k) for k in (0, 1)]
    if q is None:
        return u0, q0
    x, y, ax, ky = [choose(which, ats, lev, JOIN_COEFS, k) for k in (5, 6, 7, 8)]
    return u0 + y * top + ax * q, q0 + x * q - ky * top


def descend(levs, values, mine_out, send_out):
    core, z, y, _ = place()
    q = top = None
    for stage, index in ((2, y), (1, z)):
        lev, value = levs[stage], values[stage]
        mid_top, mid_q = inside(lev, value, 0, (2,), q, top)
        if q is None:
            q = top = jnp.zeros_like(mid_q)
        high = index >= 2
        q, top = jnp.where(high, mid_q, q), jnp.where(high, top, mid_top)
        mid_top, mid_q = inside(lev, value, lax.div(index, 2), (0, 1), q, top)
        odd = lax.rem(index, 2) == 1
        q, top = jnp.where(odd, mid_q, q), jnp.where(odd, top, mid_top)
    mid_top, mid_q = inside(levs[0], values[0], 0, (0,), q, top)
    upper = core == 1
    put(mine_out, 0, jnp.where(upper, mid_q, q))
    put(mine_out, 1, jnp.where(upper, top, mid_top))
    put(send_out, 0, jnp.where(upper, q, mid_q))
    put(send_out, 1, jnp.where(upper, mid_top, top))


def descend_border(levs, mine_out, send_out):
    core, z, y, _ = place()
    lo = hi = jnp.zeros_like(mine_out[4, 0:1])

    def flux(lev, which, ats):
        f, k1, k2 = [pick(which, [lev[j, k:k + 1] for j in ats]) for k in range(3)]
        return f + k2 * hi - k1 * lo

    for stage, index in ((2, y), (1, z)):
        f = flux(levs[stage], 0, (2,))
        high = index >= 2
        lo, hi = jnp.where(high, -f, lo), jnp.where(high, hi, f)
        f = flux(levs[stage], lax.div(index, 2), (0, 1))
        odd = lax.rem(index, 2) == 1
        lo, hi = jnp.where(odd, -f, lo), jnp.where(odd, hi, f)
    f = flux(levs[0], 0, (0,))
    upper = core == 1
    mine_out[4], send_out[4] = jnp.zeros_like(mine_out[4]), jnp.zeros_like(send_out[4])
    mine_out[4, 0:1], mine_out[4, 1:2] = jnp.where(upper, -f, lo), jnp.where(upper, hi, f)
    send_out[4, 0:1], send_out[4, 1:2] = jnp.where(upper, lo, -f), jnp.where(upper, f, hi)


def first_last_kernel(count, mine, *refs):
    received = refs[:count]
    lev0, lev1, val0, val1, blev0, blev1, mine_out, send_out, lev2, val2, blev2 = refs[count:]
    index = stage_index(2)
    stage_coefs(index, mine, received, lev2)
    stage_rhs(index, mine, received, lev2, val2)
    stage_border(index, mine, received, blev2)
    descend((lev0, lev1, lev2), (val0, val1, val2), mine_out, send_out)
    descend_border((blev0, blev1, blev2), mine_out, send_out)


def second_last_kernel(count, mine, *refs):
    received = refs[:count]
    lev0, lev1, lev2, val0, val1, mine_out, send_out, val2 = refs[count:]
    stage_rhs(stage_index(2), mine, received, lev2, val2)
    descend((lev0, lev1, lev2), (val0, val1, val2), mine_out, send_out)


def whole_ports(own, other):
    second = place()[3] == 1
    planes = []
    for k in (0, 1):
        low = [jnp.where(second, other[2 * k + t], own[2 * k + t]) for t in (0, 1)]
        high = [jnp.where(second, own[2 * k + t], other[2 * k + t]) for t in (0, 1)]
        planes.append(low + high)
    return planes


def split_cols(tile):
    return [tile[:, c:c + 128] for c in range(0, tile.shape[-1], 128)]


def middle_kernel(
    rows, slab, cols,
    own, other, s_ref, g_ref, r_ref, gp_ref, fwd_in, last_ref, keep_ref, source_ref, ssum_ref, border_ref,
    fwd_ref, mine_ref, send_ref, ports_ref,
):
    q, u = whole_ports(own, other)
    inflow = jnp.concatenate(q, axis=0)
    u = jnp.concatenate(u, axis=0)
    row = lax.broadcasted_iota(jnp.int32, (8, cols), 0)
    second = place()[3] == 1
    low_tile, high_tile = jnp.where(second, other[4], own[4]), jnp.where(second, own[4], other[4])
    inflow_b = jnp.where(row == 7, low_tile[0:1], high_tile[0:1])
    top_b = jnp.where(row == 7, low_tile[1:2], high_tile[1:2])
    narrow = lax.broadcasted_iota(jnp.int32, (8, 128), 0)
    last = slab // 8 - 1
    for z in range(rows - 1, -1, -1):
        r = r_ref[z] if z < rows - 1 else last_ref[1]
        g = g_ref[z] if z < rows - 1 else last_ref[0]
        u = r * (fwd_in[z] + gp_ref[z] * inflow) + g * u
        state = source_ref[z] + keep_ref[z] * u
        sb, gb, rb, gpb, fb, keep_b, source_b = [border_ref[k, z] for k in range(7)]
        rhs = fb + gpb * inflow_b
        ub = rb * (rhs + top_b) if z == rows - 1 else rb * rhs + gb * ub
        flow_b = split_cols(sb * (source_b + keep_b * ub))
        sb = split_cols(sb)
        state = [split_cols(tile_of(state, t)) for t in range(slab // 8)]
        s, ssum = tiles_of(s_ref, z, slab, cols), tiles_of(ssum_ref, z, slab, cols)
        ssum[0] = [x + jnp.where(narrow == 0, pltpu.roll(y, 1, 0), 0.0) for x, y in zip(ssum[0], sb)]
        ssum[last] = [x + jnp.where(narrow == 7, pltpu.roll(y, 7, 0), 0.0) for x, y in zip(ssum[last], sb)]
        vsum = neighbour_sum([[x * y for x, y in zip(*lines)] for lines in zip(s, state)], flow_b)
        for t in range(slab // 8):
            for c in range(cols // 128):
                fwd_ref[z, 8 * t:8 * t + 8, 128 * c:128 * c + 128] = state[t][c] + SECTION_RATE * s[t][c] * (
                    vsum[t][c] - state[t][c] * ssum[t][c])
    e = fwd_ref[0]
    total = gp_ref[0] * r_ref[0] * e
    for z in range(1, rows):
        e = fwd_ref[z] + g_ref[z - 1] * e
        fwd_ref[z] = e
        total = total + gp_ref[z] * (r_ref[z] if z < rows - 1 else last_ref[1]) * e
    ports_ref[0] = total
    ports_ref[1] = last_ref[0] * e
    half = place()[3]
    split_ports(slab, 2, ports_ref, mine_ref, half)
    split_ports(slab, 2, ports_ref, send_ref, 1 - half)


def final_kernel(
    rows, slab,
    own, other, g_ref, r_ref, gp_ref, fwd_ref, last_ref, keep_ref, source_ref,
    out_hbm, out, sems,
):
    q, u = [jnp.concatenate(tiles, axis=0) for tiles in whole_ports(own, other)]
    copies = []
    for z in range(rows - 1, -1, -1):
        r = r_ref[z] if z < rows - 1 else last_ref[1]
        g = g_ref[z] if z < rows - 1 else last_ref[0]
        u = r * (fwd_ref[z] + gp_ref[z] * q) + g * u
        out[z] = source_ref[z] + keep_ref[z] * u
        if z % CHUNK == 0:
            here = pl.ds(z, CHUNK)
            copy = pltpu.make_async_copy(out.at[here], out_hbm.at[here], sems.at[z // CHUNK])
            copy.start()
            copies.append(copy)
    for copy in copies:
        copy.wait()


def on_device(partners, concentration, tissue_mask, wall_layer, stiffness, production, layer_diffusivity, uptake_rate):
    rows, slab, cols = concentration.shape
    nx, nax = lax.axis_size("xs"), lax.axis_size("ax")
    block = (rows, slab, cols)
    smem = pl.BlockSpec(memory_space=pltpu.SMEM)
    hbm = pl.BlockSpec(memory_space=pltpu.HBM)

    def in_hbm(x):
        return pltpu.with_memory_space_constraint(x, pltpu.HBM)

    def call(kernel, outs, operands, scratch=(), specs=None, out_specs=None, us=1.0):
        return pl.pallas_call(
            kernel,
            out_shape=outs,
            in_specs=specs or [vspec()] * len(operands),
            out_specs=out_specs or [vspec()] * len(outs),
            scratch_shapes=list(scratch),
            compiler_params=params(),
            cost_estimate=cost(us),
        )(*operands)

    def exchange(block, stage):
        received = {step: lax.ppermute(block, "ax", route) for step, route in partners[stage]}
        return [received[step] for step in sorted(received)]

    def f32(*shape):
        return pltpu.VMEM(shape, jnp.float32)

    def i32(*shape):
        return pltpu.VMEM(shape, jnp.int32)

    conc, mask, layer, stiff, prod = [
        in_hbm(x) for x in (concentration, tissue_mask, wall_layer, stiffness, production)]
    diff_table, uptake_rate = in_hbm(layer_diffusivity), in_hbm(uptake_rate)
    lo, hi, first_s = call(
        functools.partial(edge_kernel, slab, cols),
        [at_vmem(5, rows, cols), at_vmem(5, rows, cols), at_vmem(slab, cols)],
        [diff_table, uptake_rate, conc, mask, layer, stiff, prod],
        scratch=[i32(2, 2, rows, cols), i32(2, 2, rows, cols), f32(2, 5, rows, cols),
                 i32(slab, cols), i32(slab, cols), f32(slab, cols),
                 pltpu.SemaphoreType.DMA((2, 9)), pltpu.SemaphoreType.DMA((3,))],
        specs=[smem, smem] + [hbm] * 5,
    )
    from_lo = lax.ppermute(hi, "xs", [(i, (i + 1) % nx) for i in range(nx)])
    from_hi = lax.ppermute(lo, "xs", [((i + 1) % nx, i) for i in range(nx)])
    above_s = lax.ppermute(first_s, "ax", [((i + 1) % nax, i) for i in range(nax)])

    s, g, r, gp, ssum, part, ends = call(
        functools.partial(setup_kernel, rows, slab, cols),
        [at_vmem(*block)] * 6 + [at_vmem(2, slab, cols)],
        [diff_table, conc, mask, layer, stiff],
        scratch=[f32(*block), i32(*block), i32(*block), f32(*block), pltpu.SemaphoreType.DMA((4, rows // CHUNK))],
        specs=[smem] + [hbm] * 4,
        us=5.0,
    )
    stack, pair = 2 * PLANES + 1, (5, 8, cols)
    fwd, last, mine, send, border = call(
        functools.partial(first_forward_kernel, rows, slab, cols, nx, nax),
        [at_vmem(*block), at_vmem(2, slab, cols), at_vmem(stack, 8, cols), at_vmem(stack, 8, cols),
         at_vmem(7, rows, 8, cols)],
        [lo, hi, s, g, r, gp, part, ends, from_lo, from_hi, above_s],
        scratch=[f32(PLANES, slab, cols), f32(2, 8, cols), f32(2, 6, rows, cols)],
    )
    levs, values, border_levs = [], [], []
    for stage in (0, 1):
        received = exchange(mine if stage else send, stage)
        joins = len(received)
        if stage == 1:
            uptake_late, mine = lax.optimization_barrier((uptake_rate, mine))
            keep, source = call(
                functools.partial(reaction_kernel, rows),
                [at_vmem(*block)] * 2,
                [uptake_late, mask, layer, prod],
                scratch=[i32(*block), i32(*block), f32(*block), pltpu.SemaphoreType.DMA((3, rows // CHUNK))],
                specs=[smem] + [hbm] * 3,
                us=2.0,
            )
            mine, keep, source = lax.optimization_barrier((mine, keep, source))
        mine, lev, value, border_lev = call(
            functools.partial(first_join_kernel, stage, joins),
            [at_vmem(stack, 8, cols), at_vmem(2 * JOIN_COEFS * joins, 8, cols), at_vmem(4 * joins, 8, cols),
             at_vmem(joins, 8, cols)],
            [mine, *received],
        )
        levs.append(lev)
        values.append(value)
        border_levs.append(border_lev)
    received = exchange(mine, 2)
    joins = len(received)
    own, send, lev = call(
        functools.partial(first_last_kernel, joins),
        [at_vmem(*pair), at_vmem(*pair), at_vmem(2 * JOIN_COEFS * joins, 8, cols)],
        [mine, *received, *levs, *values, *border_levs],
        scratch=[f32(4 * joins, 8, cols), f32(joins, 8, cols)],
    )
    levs.append(lev)
    (other,) = exchange(send, 0)

    fwd, mine, send = call(
        functools.partial(middle_kernel, rows, slab, cols),
        [at_vmem(*block), at_vmem(4, 8, cols), at_vmem(4, 8, cols)],
        [own, other, s, g, r, gp, fwd, last, keep, source, ssum, border],
        scratch=[f32(2, slab, cols)],
        us=3.0,
    )
    values = []
    for stage in (0, 1):
        received = exchange(mine if stage else send, stage)
        joins = len(received)
        mine, value = call(
            functools.partial(second_join_kernel, stage, joins),
            [at_vmem(4, 8, cols), at_vmem(4 * joins, 8, cols)],
            [mine, *received, levs[stage]],
        )
        values.append(value)
    received = exchange(mine, 2)
    joins = len(received)
    own, send = call(
        functools.partial(second_last_kernel, joins),
        [at_vmem(4, 8, cols), at_vmem(4, 8, cols)],
        [mine, *received, *levs, *values],
        scratch=[f32(4 * joins, 8, cols)],
    )
    (other,) = exchange(send, 0)
    (out,) = call(
        functools.partial(final_kernel, rows, slab),
        [jax.ShapeDtypeStruct(block, jnp.float32)],
        [own, other, g, r, gp, fwd, last, keep, source],
        scratch=[f32(*block), pltpu.SemaphoreType.DMA((rows // CHUNK,))],
        out_specs=[hbm],
    )
    return out


def join_partners():
    stages = (
        ((1, lambda y, z, c: (y, z, 1 - c)),),
        tuple((k, lambda y, z, c, k=k: (y, z ^ k, c ^ (k & 1))) for k in ORDER),
        tuple((k, lambda y, z, c, k=k: (y ^ k, z, c ^ (k & 1))) for k in ORDER),
    )
    routes = []
    for flips in stages:
        routes.append([])
        for step, flip in flips:
            route = []
            for i in range(32):
                y, z, c = flip(i // 8, i // 2 % 4, i % 2)
                route.append((i, y * 8 + z * 2 + c))
            routes[-1].append((step, route))
    return routes


def solution(mesh):
    placed = (P("ax", "xs", None),) * 5 + (P(), P())
    return jax.shard_map(
        functools.partial(on_device, join_partners()),
        mesh=mesh, in_specs=placed, out_specs=P("ax", "xs", None), check_vma=False,
    )
```

```python
import functools

import jax
import jax.numpy as jnp
from jax import lax
from jax.experimental import pallas as pl
from jax.experimental.pallas import tpu as pltpu
from jax.sharding import PartitionSpec as P

RZ = 3072.0
SECTION_RATE = 0.05
LAYERS = 4
LIMIT = 24 * 1024 * 1024
CHUNK = 8
PLANES = 5
JOIN_COEFS = 9
ORDER = (1, 3, 2)


def at_vmem(*shape):
    return pltpu.VMEM(shape, jnp.float32)


def vspec():
    return pl.BlockSpec(memory_space=pltpu.VMEM)


def params():
    return pltpu.CompilerParams(vmem_limit_bytes=LIMIT)


def cost(us):
    return pl.CostEstimate(flops=int(us * 2e6), bytes_accessed=int(us * 3e6), transcendentals=0)


def lookup(labels, table):
    value = table[LAYERS - 1]
    for layer in range(LAYERS - 1):
        value = jnp.where(labels == layer, table[layer], value)
    return value


def root_diffusivity(mask, layer, stiff, table):
    inside = lookup(layer, table) * stiff
    return jnp.where(mask == 0, 0.0, inside * lax.rsqrt(inside))


def inverse(x):
    return pl.reciprocal(x, approx=True)


def tiles_of(ref, z, slab, cols):
    return [[ref[z, t:t + 8, c:c + 128] for c in range(0, cols, 128)] for t in range(0, slab, 8)]


def neighbour_sum(tiles, border=None):
    rows, cols = len(tiles), len(tiles[0])
    row = lax.broadcasted_iota(jnp.int32, (8, 128), 0)
    lane = lax.broadcasted_iota(jnp.int32, (8, 128), 1)

    def rolled(shift, axis):
        return [[pltpu.roll(tile, shift, axis) for tile in line] for line in tiles]

    down, up, right, left = rolled(1, 0), rolled(7, 0), rolled(1, 1), rolled(127, 1)
    if border is not None:
        down.append([pltpu.roll(tile, 1, 0) for tile in border])
        up.append([pltpu.roll(tile, 7, 0) for tile in border])

    def at(array, t, c):
        if 0 <= c < cols and 0 <= t < rows:
            return array[t][c]
        return 0.0 if border is None or not 0 <= c < cols else array[rows][c]

    return [[
        (jnp.where(row == 0, at(down, t - 1, c), down[t][c]) + jnp.where(row == 7, at(up, t + 1, c), up[t][c]))
        + (jnp.where(lane == 0, at(right, t, c - 1), right[t][c])
           + jnp.where(lane == 127, at(left, t, c + 1), left[t][c]))
        for c in range(cols)] for t in range(rows)]


def along_cols(plane):
    cols = plane.shape[-1]
    lane = lax.broadcasted_iota(jnp.int32, plane.shape, 1)
    return (jnp.where(lane == 0, 0.0, pltpu.roll(plane, 1, 1))
            + jnp.where(lane == cols - 1, 0.0, pltpu.roll(plane, cols - 1, 1)))


def read_table(table):
    return [table[k] for k in range(LAYERS)]


def edge_kernel(
    slab, cols,
    diff_table, conc_hbm, mask_hbm, layer_hbm, stiff_hbm,
    lo_out, hi_out, first_out,
    mask, layer, floats, mask_row, layer_row, stiff_row, sems, row_sems,
):
    copies = []
    for side in (0, 1):
        sources = []
        for depth in (0, 1):
            x = depth if side == 0 else slab - 1 - depth
            sources += [(mask_hbm.at[:, x], mask.at[side, depth]), (layer_hbm.at[:, x], layer.at[side, depth]),
                        (stiff_hbm.at[:, x], floats.at[side, depth]), (conc_hbm.at[:, x], floats.at[side, 2 + depth])]
        copies.append([
            pltpu.make_async_copy(source, target, sems.at[side, k]) for k, (source, target) in enumerate(sources)])
    copies.append([
        pltpu.make_async_copy(source.at[0], target, row_sems.at[k])
        for k, (source, target) in enumerate(((mask_hbm, mask_row), (layer_hbm, layer_row), (stiff_hbm, stiff_row)))])
    for group in copies:
        for copy in group:
            copy.start()
    table = read_table(diff_table)
    for side, out in ((0, lo_out), (1, hi_out)):
        for copy in copies[side]:
            copy.wait()
        s, inner = [root_diffusivity(mask[side, d], layer[side, d], floats[side, d], table) for d in (0, 1)]
        state = floats[side, 2]
        ssum = inner + along_cols(s)
        vsum = inner * floats[side, 3] + along_cols(s * state)
        out[0] = s
        out[1] = state
        out[2] = state + SECTION_RATE * s * (vsum - state * ssum)
    for copy in copies[2]:
        copy.wait()
    first_out[...] = root_diffusivity(mask_row[...], layer_row[...], stiff_row[...], table)


def setup_kernel(
    rows, slab, cols,
    table, conc, mask, layer, stiff,
    s_out, g_out, r_out, gp_out, ssum_out, part_out, ends_out,
):
    weights = read_table(table)
    grid = [(t, c) for t in range(slab // 8) for c in range(cols // 128)]
    s = m = gp = alpha = None
    for z in range(rows):
        w, lab, sti, st = [tiles_of(ref, z, slab, cols) for ref in (mask, layer, stiff, conc)]
        s_next = [[root_diffusivity(w[t][c], lab[t][c], sti[t][c], weights)
                   for c in range(cols // 128)] for t in range(slab // 8)]
        flow = [[s_next[t][c] * st[t][c] for c in range(cols // 128)] for t in range(slab // 8)]
        ssum, vsum = neighbour_sum(s_next), neighbour_sum(flow)
        for t, c in grid:
            here = (z, pl.ds(8 * t, 8), pl.ds(128 * c, 128))
            s_out[here] = s_next[t][c]
            ssum_out[here] = ssum[t][c]
            part_out[here] = st[t][c] + SECTION_RATE * s_next[t][c] * (vsum[t][c] - st[t][c] * ssum[t][c])
        if z == 0:
            ones = {k: jnp.ones((8, 128), jnp.float32) for k in grid}
            m, gp, alpha = dict(ones), dict(ones), {k: jnp.zeros((8, 128), jnp.float32) for k in grid}
        else:
            for t, c in grid:
                k = (t, c)
                here = (z - 1, pl.ds(8 * t, 8), pl.ds(128 * c, 128))
                couple = RZ * s[t][c] * s_next[t][c]
                r = inverse(m[k] + couple)
                g = couple * r
                r_out[here] = r
                g_out[here] = g
                gp_out[here] = gp[k]
                alpha[k] = alpha[k] + r * (gp[k] * gp[k])
                m[k] = 1.0 + g * m[k]
                gp[k] = gp[k] * g
        s = s_next
    for t, c in grid:
        here = (pl.ds(8 * t, 8), pl.ds(128 * c, 128))
        gp_out[(rows - 1,) + here] = gp[t, c]
        ends_out[(0,) + here] = m[t, c]
        ends_out[(1,) + here] = alpha[t, c]


def reaction_kernel(rows, uptake_table, mask, layer, prod, keep_out, source_out, lo_out, hi_out):
    tab = read_table(uptake_table)
    for z in range(rows):
        weight = mask[z].astype(jnp.float32)
        keep = 1.0 - weight * lookup(layer[z], tab)
        source = weight * prod[z]
        keep_out[z] = keep
        source_out[z] = source
        lo_out[0, z:z + 1] = keep[0:1]
        lo_out[1, z:z + 1] = source[0:1]
        hi_out[0, z:z + 1] = keep[-1:]
        hi_out[1, z:z + 1] = source[-1:]


def tile_of(tiles, k):
    return tiles[8 * k:8 * k + 8]


def first_forward_kernel(
    rows, slab, cols, nx, nax,
    own_lo, own_hi, s_ref, g_ref, r_ref, gp_ref, part_ref, ends_ref, from_lo, from_hi, above_ref,
    fwd_ref, last_ref, mine_ref, send_ref, border_ref,
    ports_ref, border_ports, lines,
):
    ix, ia = lax.axis_index("xs"), lax.axis_index("ax")
    above = jnp.where(ia < nax - 1, RZ, 0.0)
    c = above * s_ref[rows - 1] * above_ref[...]
    m, alpha = ends_ref[0], ends_ref[1]
    last_r = inverse(m + c)
    last_g = c * last_r
    gp = gp_ref[rows - 1]
    last_ref[0] = last_g
    last_ref[1] = last_r
    ports_ref[2] = alpha + last_r * gp * gp
    ports_ref[3] = last_g * gp
    ports_ref[4] = last_g * m

    for side, (own, halo, exists) in enumerate(((own_lo, from_lo, ix > 0), (own_hi, from_hi, ix < nx - 1))):
        s_own, state_own = own[0], own[1]
        s = jnp.where(exists, halo[0], 0.0)
        state = halo[1]
        flux = SECTION_RATE * s_own * s * (state - state_own)
        lines[side, 0] = s
        lines[side, 1] = halo[2] - flux
        lines[side, 2] = RZ * s * pltpu.roll(s, rows - 1, 0)
        lines[side, 3] = flux

    row = lax.broadcasted_iota(jnp.int32, (8, cols), 0)
    is_lo = row == 7

    def border(k, z):
        return jnp.where(is_lo, lines[0, k, z:z + 1], lines[1, k, z:z + 1])

    total = prev = None
    for z in range(rows):
        part = part_ref[z]
        edges = (jnp.where(row == 0, lines[0, 3, z:z + 1], 0.0), jnp.where(row == 7, lines[1, 3, z:z + 1], 0.0))
        e = jnp.concatenate([part[0:8] + edges[0], part[8:slab - 8], part[slab - 8:] + edges[1]], axis=0)
        if z > 0:
            e = e + g_ref[z - 1] * prev
        fwd_ref[z] = e
        term = gp_ref[z] * (r_ref[z] if z < rows - 1 else last_r) * e
        total = term if z == 0 else total + term
        prev = e

        sb, eb = border(0, z), border(1, z)
        if z == 0:
            mb = gpb = jnp.ones_like(sb)
            first = sb
        else:
            eb = eb + gb * fb
            mb = 1.0 + gb * mb
            gpb = gpb * gb
        if z < rows - 1:
            cb = border(2, z)
            rb = inverse(mb + cb)
            gb = cb * rb
        else:
            rb = inverse(mb)
            gb = jnp.zeros_like(rb)
        fb = eb
        grb = gpb * rb
        ab = grb * gpb if z == 0 else ab + grb * gpb
        pb = grb * eb if z == 0 else pb + grb * eb
        for k, value in enumerate((sb, gb, rb, gpb, fb)):
            border_ref[k, z] = value
    ports_ref[0] = total
    ports_ref[1] = last_g * prev
    zero = jnp.zeros_like(sb)
    for k, value in enumerate((ab, grb, rb, pb, rb * fb, first, sb, zero)):
        border_ports[0, k:k + 1] = value[7:8]
        border_ports[1, k:k + 1] = value[0:1]
    half = place()[3]
    for out, which in ((mine_ref, half), (send_ref, 1 - half)):
        split_ports(slab, PLANES, ports_ref, out, which)
        out[2 * PLANES] = border_ports[which]


def split_ports(slab, planes, ports_ref, out, which):
    for t in range(slab // 16):
        at = pl.ds(pl.multiple_of(which * (slab // 2) + 8 * t, 8), 8)
        for k in range(planes):
            out[2 * k + t] = ports_ref[k, at]


def place():
    i = lax.axis_index("ax")
    core, z, y = lax.rem(i, 2), lax.rem(lax.div(i, 2), 4), lax.div(i, 8)
    return core, z, y, lax.rem(core + z + y, 2)


def pick(index, options):
    value = options[0]
    for k in range(1, len(options)):
        value = jnp.where(index == k, options[k], value)
    return value


def ordered(index, mine, received):
    options = [mine] + [received[ORDER.index(step)] for step in range(1, 1 + len(received))] if len(received) > 1 else [mine, *received]
    return [pick(index ^ j, options) for j in range(1 + len(received))]


def main_planes(stack, planes):
    return [stack[2 * k:2 * k + 2] for k in planes]


def put(stack, at, value):
    stack[2 * at:2 * at + 2] = value


def join_coefs(low, high, lev, at):
    (alpha1, beta1, kappa1), (alpha2, beta2, kappa2) = low, high
    rho = inverse(1.0 + kappa1 * alpha2)
    x, y = beta1 * rho, beta2 * rho
    ax, ky = alpha2 * x, kappa1 * y
    for k, value in enumerate((rho, kappa1, alpha2, beta1, beta2, x, y, ax, ky)):
        put(lev, at * JOIN_COEFS + k, value)
    return alpha1 + beta1 * ax, x * beta2, kappa2 + beta2 * ky


def join_rhs(low, high, lev, at, values):
    (a1, b1), (a2, b2) = low, high
    rho, kappa1, alpha2, beta1, beta2 = main_planes(lev, range(at * JOIN_COEFS, at * JOIN_COEFS + 5))
    u0 = rho * (a2 + alpha2 * b1)
    q0 = rho * (b1 - kappa1 * a2)
    put(values, 2 * at, u0)
    put(values, 2 * at + 1, q0)
    return a1 + beta1 * u0, b2 + beta2 * q0


def join_border(low, high, lev, at):
    (a1, b1, d1, first1, last1, s_first, s1), (a2, b2, d2, first2, last2, s2, s_last) = low, high
    c = RZ * s1 * s2
    k = c * inverse(1.0 + c * (a2 + d1))
    f, k1, k2 = k * (first2 - last1), k * b1, k * b2
    for j, value in enumerate((f, k1, k2)):
        lev[at, j:j + 1] = value
    return a1 - k1 * b1, k1 * b2, d2 - k2 * b2, first1 + b1 * f, last2 - b2 * f, s_first, s_last


def join_all(groups, join):
    if len(groups) == 2:
        return join(groups[0], groups[1], 0)
    return join(join(groups[0], groups[1], 0), join(groups[2], groups[3], 1), 2)


def stage_coefs(index, mine, received, lev):
    stacks = [main_planes(stack, (2, 3, 4)) for stack in (mine, *received)]
    planes = [ordered(index, own[0], list(own[1:])) for own in zip(*stacks)]
    return join_all(list(zip(*planes)), lambda low, high, at: join_coefs(low, high, lev, at))


def stage_rhs(index, mine, received, lev, values):
    stacks = [main_planes(stack, (0, 1)) for stack in (mine, *received)]
    planes = [ordered(index, own[0], list(own[1:])) for own in zip(*stacks)]
    return join_all(list(zip(*planes)), lambda low, high, at: join_rhs(low, high, lev, at, values))


def stage_border(index, mine, received, lev):
    tiles = ordered(index, mine[2 * PLANES], [stack[2 * PLANES] for stack in received])
    groups = [[tile[k:k + 1] for k in range(7)] for tile in tiles]
    return join_all(groups, lambda low, high, at: join_border(low, high, lev, at))


def stage_index(stage):
    return place()[stage]


def first_join_kernel(stage, count, mine, *refs):
    received, (out, lev, values, border_lev) = refs[:count], refs[count:]
    index = stage_index(stage)
    for k, value in zip((2, 3, 4), stage_coefs(index, mine, received, lev)):
        put(out, k, value)
    for k, value in zip((0, 1), stage_rhs(index, mine, received, lev, values)):
        put(out, k, value)
    for k, value in enumerate(stage_border(index, mine, received, border_lev)):
        out[2 * PLANES, k:k + 1] = value
    out[2 * PLANES, 7:8] = jnp.zeros_like(value)


def second_join_kernel(stage, count, mine, *refs):
    received, (lev, out, values) = refs[:count], refs[count:]
    for k, value in zip((0, 1), stage_rhs(stage_index(stage), mine, received, lev, values)):
        put(out, k, value)


def choose(which, ats, stack, width, k):
    return pick(which, [stack[2 * (j * width + k):2 * (j * width + k) + 2] for j in ats])


def inside(lev, values, which, ats, q, top):
    u0, q0 = [choose(which, ats, values, 2, k) for k in (0, 1)]
    if q is None:
        return u0, q0
    x, y, ax, ky = [choose(which, ats, lev, JOIN_COEFS, k) for k in (5, 6, 7, 8)]
    return u0 + y * top + ax * q, q0 + x * q - ky * top


def descend(levs, values, mine_out, send_out):
    core, z, y, _ = place()
    q = top = None
    for stage, index in ((2, y), (1, z)):
        lev, value = levs[stage], values[stage]
        mid_top, mid_q = inside(lev, value, 0, (2,), q, top)
        if q is None:
            q = top = jnp.zeros_like(mid_q)
        high = index >= 2
        q, top = jnp.where(high, mid_q, q), jnp.where(high, top, mid_top)
        mid_top, mid_q = inside(lev, value, lax.div(index, 2), (0, 1), q, top)
        odd = lax.rem(index, 2) == 1
        q, top = jnp.where(odd, mid_q, q), jnp.where(odd, top, mid_top)
    mid_top, mid_q = inside(levs[0], values[0], 0, (0,), q, top)
    upper = core == 1
    put(mine_out, 0, jnp.where(upper, mid_q, q))
    put(mine_out, 1, jnp.where(upper, top, mid_top))
    put(send_out, 0, jnp.where(upper, q, mid_q))
    put(send_out, 1, jnp.where(upper, mid_top, top))


def descend_border(levs, mine_out, send_out):
    core, z, y, _ = place()
    lo = hi = jnp.zeros_like(mine_out[4, 0:1])

    def flux(lev, which, ats):
        f, k1, k2 = [pick(which, [lev[j, k:k + 1] for j in ats]) for k in range(3)]
        return f + k2 * hi - k1 * lo

    for stage, index in ((2, y), (1, z)):
        f = flux(levs[stage], 0, (2,))
        high = index >= 2
        lo, hi = jnp.where(high, -f, lo), jnp.where(high, hi, f)
        f = flux(levs[stage], lax.div(index, 2), (0, 1))
        odd = lax.rem(index, 2) == 1
        lo, hi = jnp.where(odd, -f, lo), jnp.where(odd, hi, f)
    f = flux(levs[0], 0, (0,))
    upper = core == 1
    mine_out[4], send_out[4] = jnp.zeros_like(mine_out[4]), jnp.zeros_like(send_out[4])
    mine_out[4, 0:1], mine_out[4, 1:2] = jnp.where(upper, -f, lo), jnp.where(upper, hi, f)
    send_out[4, 0:1], send_out[4, 1:2] = jnp.where(upper, lo, -f), jnp.where(upper, f, hi)


def first_last_kernel(count, mine, *refs):
    received = refs[:count]
    lev0, lev1, val0, val1, blev0, blev1, mine_out, send_out, lev2, val2, blev2 = refs[count:]
    index = stage_index(2)
    stage_coefs(index, mine, received, lev2)
    stage_rhs(index, mine, received, lev2, val2)
    stage_border(index, mine, received, blev2)
    descend((lev0, lev1, lev2), (val0, val1, val2), mine_out, send_out)
    descend_border((blev0, blev1, blev2), mine_out, send_out)


def second_last_kernel(count, mine, *refs):
    received = refs[:count]
    lev0, lev1, lev2, val0, val1, mine_out, send_out, val2 = refs[count:]
    stage_rhs(stage_index(2), mine, received, lev2, val2)
    descend((lev0, lev1, lev2), (val0, val1, val2), mine_out, send_out)


def whole_ports(own, other):
    second = place()[3] == 1
    planes = []
    for k in (0, 1):
        low = [jnp.where(second, other[2 * k + t], own[2 * k + t]) for t in (0, 1)]
        high = [jnp.where(second, own[2 * k + t], other[2 * k + t]) for t in (0, 1)]
        planes.append(low + high)
    return planes


def split_cols(tile):
    return [tile[:, c:c + 128] for c in range(0, tile.shape[-1], 128)]


def middle_kernel(
    rows, slab, cols,
    own, other, s_ref, g_ref, r_ref, gp_ref, fwd_in, last_ref, keep_ref, source_ref, ssum_ref, border_ref,
    reaction_lo, reaction_hi,
    fwd_ref, mine_ref, send_ref, ports_ref,
):
    q, u = whole_ports(own, other)
    inflow = jnp.concatenate(q, axis=0)
    u = jnp.concatenate(u, axis=0)
    row = lax.broadcasted_iota(jnp.int32, (8, cols), 0)
    second = place()[3] == 1
    low_tile, high_tile = jnp.where(second, other[4], own[4]), jnp.where(second, own[4], other[4])
    inflow_b = jnp.where(row == 7, low_tile[0:1], high_tile[0:1])
    top_b = jnp.where(row == 7, low_tile[1:2], high_tile[1:2])
    narrow = lax.broadcasted_iota(jnp.int32, (8, 128), 0)
    last = slab // 8 - 1
    for z in range(rows - 1, -1, -1):
        r = r_ref[z] if z < rows - 1 else last_ref[1]
        g = g_ref[z] if z < rows - 1 else last_ref[0]
        u = r * (fwd_in[z] + gp_ref[z] * inflow) + g * u
        state = source_ref[z] + keep_ref[z] * u
        sb, gb, rb, gpb, fb = [border_ref[k, z] for k in range(5)]
        keep_b, source_b = [jnp.where(row == 7, reaction_lo[k, z:z + 1], reaction_hi[k, z:z + 1]) for k in (0, 1)]
        rhs = fb + gpb * inflow_b
        ub = rb * (rhs + top_b) if z == rows - 1 else rb * rhs + gb * ub
        flow_b = split_cols(sb * (source_b + keep_b * ub))
        sb = split_cols(sb)
        state = [split_cols(tile_of(state, t)) for t in range(slab // 8)]
        s, ssum = tiles_of(s_ref, z, slab, cols), tiles_of(ssum_ref, z, slab, cols)
        ssum[0] = [x + jnp.where(narrow == 0, pltpu.roll(y, 1, 0), 0.0) for x, y in zip(ssum[0], sb)]
        ssum[last] = [x + jnp.where(narrow == 7, pltpu.roll(y, 7, 0), 0.0) for x, y in zip(ssum[last], sb)]
        vsum = neighbour_sum([[x * y for x, y in zip(*lines)] for lines in zip(s, state)], flow_b)
        for t in range(slab // 8):
            for c in range(cols // 128):
                fwd_ref[z, 8 * t:8 * t + 8, 128 * c:128 * c + 128] = state[t][c] + SECTION_RATE * s[t][c] * (
                    vsum[t][c] - state[t][c] * ssum[t][c])
    e = fwd_ref[0]
    total = gp_ref[0] * r_ref[0] * e
    for z in range(1, rows):
        e = fwd_ref[z] + g_ref[z - 1] * e
        fwd_ref[z] = e
        total = total + gp_ref[z] * (r_ref[z] if z < rows - 1 else last_ref[1]) * e
    ports_ref[0] = total
    ports_ref[1] = last_ref[0] * e
    half = place()[3]
    split_ports(slab, 2, ports_ref, mine_ref, half)
    split_ports(slab, 2, ports_ref, send_ref, 1 - half)


def final_kernel(
    rows, slab,
    own, other, g_ref, r_ref, gp_ref, fwd_ref, last_ref, keep_ref, source_ref,
    out_hbm, out, sems,
):
    q, u = [jnp.concatenate(tiles, axis=0) for tiles in whole_ports(own, other)]
    copies = []
    for z in range(rows - 1, -1, -1):
        r = r_ref[z] if z < rows - 1 else last_ref[1]
        g = g_ref[z] if z < rows - 1 else last_ref[0]
        u = r * (fwd_ref[z] + gp_ref[z] * q) + g * u
        out[z] = source_ref[z] + keep_ref[z] * u
        if z % CHUNK == 0:
            here = pl.ds(z, CHUNK)
            copy = pltpu.make_async_copy(out.at[here], out_hbm.at[here], sems.at[z // CHUNK])
            copy.start()
            copies.append(copy)
    for copy in copies:
        copy.wait()


def on_device(partners, concentration, tissue_mask, wall_layer, stiffness, production, layer_diffusivity, uptake_rate):
    rows, slab, cols = concentration.shape
    nx, nax = lax.axis_size("xs"), lax.axis_size("ax")
    block = (rows, slab, cols)
    smem = pl.BlockSpec(memory_space=pltpu.SMEM)
    hbm = pl.BlockSpec(memory_space=pltpu.HBM)

    def in_hbm(x):
        return pltpu.with_memory_space_constraint(x, pltpu.HBM)

    def call(kernel, outs, operands, scratch=(), specs=None, out_specs=None, us=1.0):
        return pl.pallas_call(
            kernel,
            out_shape=outs,
            in_specs=specs or [vspec()] * len(operands),
            out_specs=out_specs or [vspec()] * len(outs),
            scratch_shapes=list(scratch),
            compiler_params=params(),
            cost_estimate=cost(us),
        )(*operands)

    def exchange(block, stage):
        received = {step: lax.ppermute(block, "ax", route) for step, route in partners[stage]}
        return [received[step] for step, _ in partners[stage]]

    def f32(*shape):
        return pltpu.VMEM(shape, jnp.float32)

    def i32(*shape):
        return pltpu.VMEM(shape, jnp.int32)

    conc, mask, layer, stiff = [
        in_hbm(x) for x in (concentration, tissue_mask, wall_layer, stiffness)]
    diff_table, uptake_rate = in_hbm(layer_diffusivity), in_hbm(uptake_rate)
    lo, hi, first_s = call(
        functools.partial(edge_kernel, slab, cols),
        [at_vmem(3, rows, cols), at_vmem(3, rows, cols), at_vmem(slab, cols)],
        [diff_table, conc, mask, layer, stiff],
        scratch=[i32(2, 2, rows, cols), i32(2, 2, rows, cols), f32(2, 4, rows, cols),
                 i32(slab, cols), i32(slab, cols), f32(slab, cols),
                 pltpu.SemaphoreType.DMA((2, 8)), pltpu.SemaphoreType.DMA((3,))],
        specs=[smem] + [hbm] * 4,
    )
    def from_neighbours(lo, hi):
        return (lax.ppermute(hi, "xs", [(i, (i + 1) % nx) for i in range(nx)]),
                lax.ppermute(lo, "xs", [((i + 1) % nx, i) for i in range(nx)]))

    from_lo, from_hi = from_neighbours(lo, hi)
    above_s = lax.ppermute(first_s, "ax", [((i + 1) % nax, i) for i in range(nax)])

    s, g, r, gp, ssum, part, ends = call(
        functools.partial(setup_kernel, rows, slab, cols),
        [at_vmem(*block)] * 6 + [at_vmem(2, slab, cols)],
        [diff_table, concentration, tissue_mask, wall_layer, stiffness],
        specs=[smem] + [vspec()] * 4,
        us=5.0,
    )
    stack, pair = 2 * PLANES + 1, (5, 8, cols)
    fwd, last, mine, send, border = call(
        functools.partial(first_forward_kernel, rows, slab, cols, nx, nax),
        [at_vmem(*block), at_vmem(2, slab, cols), at_vmem(stack, 8, cols), at_vmem(stack, 8, cols),
         at_vmem(5, rows, 8, cols)],
        [lo, hi, s, g, r, gp, part, ends, from_lo, from_hi, above_s],
        scratch=[f32(PLANES, slab, cols), f32(2, 8, cols), f32(2, 4, rows, cols)],
    )
    levs, values, border_levs = [], [], []
    for stage in (0, 1):
        received = exchange(mine if stage else send, stage)
        joins = len(received)
        if stage == 1:
            uptake_late, mine = lax.optimization_barrier((uptake_rate, mine))
            keep, source, lo, hi = call(
                functools.partial(reaction_kernel, rows),
                [at_vmem(*block)] * 2 + [at_vmem(2, rows, cols)] * 2,
                [uptake_late, tissue_mask, wall_layer, production],
                specs=[smem] + [vspec()] * 3,
                us=2.0,
            )
            reaction_lo, reaction_hi = from_neighbours(lo, hi)
            mine, keep, source = lax.optimization_barrier((mine, keep, source))
        mine, lev, value, border_lev = call(
            functools.partial(first_join_kernel, stage, joins),
            [at_vmem(stack, 8, cols), at_vmem(2 * JOIN_COEFS * joins, 8, cols), at_vmem(4 * joins, 8, cols),
             at_vmem(joins, 8, cols)],
            [mine, *received],
        )
        levs.append(lev)
        values.append(value)
        border_levs.append(border_lev)
    received = exchange(mine, 2)
    joins = len(received)
    own, send, lev = call(
        functools.partial(first_last_kernel, joins),
        [at_vmem(*pair), at_vmem(*pair), at_vmem(2 * JOIN_COEFS * joins, 8, cols)],
        [mine, *received, *levs, *values, *border_levs],
        scratch=[f32(4 * joins, 8, cols), f32(joins, 8, cols)],
    )
    levs.append(lev)
    (other,) = exchange(send, 0)

    fwd, mine, send = call(
        functools.partial(middle_kernel, rows, slab, cols),
        [at_vmem(*block), at_vmem(4, 8, cols), at_vmem(4, 8, cols)],
        [own, other, s, g, r, gp, fwd, last, keep, source, ssum, border, reaction_lo, reaction_hi],
        scratch=[f32(2, slab, cols)],
        us=3.0,
    )
    values = []
    for stage in (0, 1):
        received = exchange(mine if stage else send, stage)
        joins = len(received)
        mine, value = call(
            functools.partial(second_join_kernel, stage, joins),
            [at_vmem(4, 8, cols), at_vmem(4 * joins, 8, cols)],
            [mine, *received, levs[stage]],
        )
        values.append(value)
    received = exchange(mine, 2)
    joins = len(received)
    own, send = call(
        functools.partial(second_last_kernel, joins),
        [at_vmem(4, 8, cols), at_vmem(4, 8, cols)],
        [mine, *received, *levs, *values],
        scratch=[f32(4 * joins, 8, cols)],
    )
    (other,) = exchange(send, 0)
    (out,) = call(
        functools.partial(final_kernel, rows, slab),
        [jax.ShapeDtypeStruct(block, jnp.float32)],
        [own, other, g, r, gp, fwd, last, keep, source],
        scratch=[f32(*block), pltpu.SemaphoreType.DMA((rows // CHUNK,))],
        out_specs=[hbm],
    )
    return out


def join_partners():
    stages = (
        ((1, lambda y, z, c: (y, z, 1 - c)),),
        tuple((k, lambda y, z, c, k=k: (y, z ^ k, c ^ (k & 1))) for k in ORDER),
        tuple((k, lambda y, z, c, k=k: (y ^ k, z, c ^ (k & 1))) for k in ORDER),
    )
    routes = []
    for flips in stages:
        routes.append([])
        for step, flip in flips:
            route = []
            for i in range(32):
                y, z, c = flip(i // 8, i // 2 % 4, i % 2)
                route.append((i, y * 8 + z * 2 + c))
            routes[-1].append((step, route))
    return routes


def solution(mesh):
    placed = (P("ax", "xs", None),) * 5 + (P(), P())
    return jax.shard_map(
        functools.partial(on_device, join_partners()),
        mesh=mesh, in_specs=placed, out_specs=P("ax", "xs", None), check_vma=False,
    )
```

```python
import functools

import jax
import jax.numpy as jnp
from jax import lax
from jax.experimental import pallas as pl
from jax.experimental.pallas import tpu as pltpu
from jax.sharding import PartitionSpec as P

RZ = 3072.0
SECTION_RATE = 0.05
LAYERS = 4
LIMIT = 24 * 1024 * 1024
CHUNK = 8
PLANES = 5
JOIN_COEFS = 9
ORDER = (1, 3, 2)


def at_vmem(*shape):
    return pltpu.VMEM(shape, jnp.float32)


def vspec():
    return pl.BlockSpec(memory_space=pltpu.VMEM)


def params():
    return pltpu.CompilerParams(vmem_limit_bytes=LIMIT)


def cost(us):
    return pl.CostEstimate(flops=int(us * 2e6), bytes_accessed=int(us * 3e6), transcendentals=0)


def lookup(labels, table):
    value = table[LAYERS - 1]
    for layer in range(LAYERS - 1):
        value = jnp.where(labels == layer, table[layer], value)
    return value


def root_diffusivity(mask, layer, stiff, table):
    inside = lookup(layer, table) * stiff
    return jnp.where(mask == 0, 0.0, inside * lax.rsqrt(inside))


def inverse(x):
    return pl.reciprocal(x, approx=True)


def tiles_of(ref, z, slab, cols):
    return [[ref[z, t:t + 8, c:c + 128] for c in range(0, cols, 128)] for t in range(0, slab, 8)]


def neighbour_sum(tiles, border=None):
    rows, cols = len(tiles), len(tiles[0])
    row = lax.broadcasted_iota(jnp.int32, (8, 128), 0)
    lane = lax.broadcasted_iota(jnp.int32, (8, 128), 1)

    def rolled(shift, axis):
        return [[pltpu.roll(tile, shift, axis) for tile in line] for line in tiles]

    down, up, right, left = rolled(1, 0), rolled(7, 0), rolled(1, 1), rolled(127, 1)
    if border is not None:
        down.append([pltpu.roll(tile, 1, 0) for tile in border])
        up.append([pltpu.roll(tile, 7, 0) for tile in border])

    def at(array, t, c):
        if 0 <= c < cols and 0 <= t < rows:
            return array[t][c]
        return 0.0 if border is None or not 0 <= c < cols else array[rows][c]

    return [[
        (jnp.where(row == 0, at(down, t - 1, c), down[t][c]) + jnp.where(row == 7, at(up, t + 1, c), up[t][c]))
        + (jnp.where(lane == 0, at(right, t, c - 1), right[t][c])
           + jnp.where(lane == 127, at(left, t, c + 1), left[t][c]))
        for c in range(cols)] for t in range(rows)]


def along_cols(plane):
    cols = plane.shape[-1]
    lane = lax.broadcasted_iota(jnp.int32, plane.shape, 1)
    return (jnp.where(lane == 0, 0.0, pltpu.roll(plane, 1, 1))
            + jnp.where(lane == cols - 1, 0.0, pltpu.roll(plane, cols - 1, 1)))


def read_table(table):
    return [table[k] for k in range(LAYERS)]


def edge_kernel(
    slab, cols,
    diff_table, conc_hbm, mask_hbm, layer_hbm, stiff_hbm,
    lo_out, hi_out, first_out,
    mask, layer, floats, mask_row, layer_row, stiff_row, sems, row_sems,
):
    copies = []
    for side in (0, 1):
        sources = []
        for depth in (0, 1):
            x = depth if side == 0 else slab - 1 - depth
            sources += [(mask_hbm.at[:, x], mask.at[side, depth]), (layer_hbm.at[:, x], layer.at[side, depth]),
                        (stiff_hbm.at[:, x], floats.at[side, depth]), (conc_hbm.at[:, x], floats.at[side, 2 + depth])]
        copies.append([
            pltpu.make_async_copy(source, target, sems.at[side, k]) for k, (source, target) in enumerate(sources)])
    copies.append([
        pltpu.make_async_copy(source.at[0], target, row_sems.at[k])
        for k, (source, target) in enumerate(((mask_hbm, mask_row), (layer_hbm, layer_row), (stiff_hbm, stiff_row)))])
    for group in copies:
        for copy in group:
            copy.start(priority=1)
    table = read_table(diff_table)
    for side, out in ((0, lo_out), (1, hi_out)):
        for copy in copies[side]:
            copy.wait()
        s, inner = [root_diffusivity(mask[side, d], layer[side, d], floats[side, d], table) for d in (0, 1)]
        state = floats[side, 2]
        ssum = inner + along_cols(s)
        vsum = inner * floats[side, 3] + along_cols(s * state)
        out[0] = s
        out[1] = state
        out[2] = state + SECTION_RATE * s * (vsum - state * ssum)
    for copy in copies[2]:
        copy.wait()
    first_out[...] = root_diffusivity(mask_row[...], layer_row[...], stiff_row[...], table)


def setup_kernel(
    rows, slab, cols,
    table, conc, mask, layer, stiff,
    s_out, g_out, r_out, gp_out, ssum_out, part_out, ends_out,
):
    weights = read_table(table)
    grid = [(t, c) for t in range(slab // 8) for c in range(cols // 128)]
    s = m = gp = alpha = None
    for z in range(rows):
        w, lab, sti, st = [tiles_of(ref, z, slab, cols) for ref in (mask, layer, stiff, conc)]
        s_next = [[root_diffusivity(w[t][c], lab[t][c], sti[t][c], weights)
                   for c in range(cols // 128)] for t in range(slab // 8)]
        flow = [[s_next[t][c] * st[t][c] for c in range(cols // 128)] for t in range(slab // 8)]
        ssum, vsum = neighbour_sum(s_next), neighbour_sum(flow)
        for t, c in grid:
            here = (z, pl.ds(8 * t, 8), pl.ds(128 * c, 128))
            s_out[here] = s_next[t][c]
            ssum_out[here] = ssum[t][c]
            part_out[here] = st[t][c] + SECTION_RATE * s_next[t][c] * (vsum[t][c] - st[t][c] * ssum[t][c])
        if z == 0:
            ones = {k: jnp.ones((8, 128), jnp.float32) for k in grid}
            m, gp, alpha = dict(ones), dict(ones), {k: jnp.zeros((8, 128), jnp.float32) for k in grid}
        else:
            for t, c in grid:
                k = (t, c)
                here = (z - 1, pl.ds(8 * t, 8), pl.ds(128 * c, 128))
                couple = RZ * s[t][c] * s_next[t][c]
                r = inverse(m[k] + couple)
                g = couple * r
                r_out[here] = r
                g_out[here] = g
                gp_out[here] = gp[k]
                alpha[k] = alpha[k] + r * (gp[k] * gp[k])
                m[k] = 1.0 + g * m[k]
                gp[k] = gp[k] * g
        s = s_next
    for t, c in grid:
        here = (pl.ds(8 * t, 8), pl.ds(128 * c, 128))
        gp_out[(rows - 1,) + here] = gp[t, c]
        ends_out[(0,) + here] = m[t, c]
        ends_out[(1,) + here] = alpha[t, c]


def reaction_kernel(rows, uptake_table, mask, layer, prod, keep_out, source_out, lo_out, hi_out):
    tab = read_table(uptake_table)
    for z in range(rows):
        weight = mask[z].astype(jnp.float32)
        keep = 1.0 - weight * lookup(layer[z], tab)
        source = weight * prod[z]
        keep_out[z] = keep
        source_out[z] = source
        lo_out[0, z:z + 1] = keep[0:1]
        lo_out[1, z:z + 1] = source[0:1]
        hi_out[0, z:z + 1] = keep[-1:]
        hi_out[1, z:z + 1] = source[-1:]


def tile_of(tiles, k):
    return tiles[8 * k:8 * k + 8]


def half_rows(slab, which):
    return pl.ds(pl.multiple_of(which * (slab // 2), slab // 2), slab // 2)


def put_rows(stack, k, value):
    stack[2 * k], stack[2 * k + 1] = value[:8], value[8:]


def half_sweep(rows, at, explicit, g_ref, r_ref, gp_ref, last_ref, fwd_ref, out):
    total = e = None
    for z in range(rows):
        e = explicit(z) if z == 0 else explicit(z) + g_ref[z - 1, at] * e
        fwd_ref[z] = e
        term = gp_ref[z, at] * (r_ref[z, at] if z < rows - 1 else last_ref[1, at]) * e
        total = term if z == 0 else total + term
    put_rows(out, 0, total)
    put_rows(out, 1, last_ref[0, at] * e)


def first_half_sweep(rows, slab, cols, which, g_ref, r_ref, gp_ref, part_ref, ends_ref, flux_ref, last_ref, fwd_ref, out):
    at = half_rows(slab, which)
    row = lax.broadcasted_iota(jnp.int32, (8, cols), 0)
    lo = jnp.where(row == jnp.where(which == 0, 0, -1), 1.0, 0.0)
    hi = jnp.where(row == jnp.where(which == 1, 7, -1), 1.0, 0.0)

    def explicit(z):
        part = part_ref[z, at]
        return jnp.concatenate(
            [part[:8] + lo * flux_ref[0, z:z + 1], part[8:] + hi * flux_ref[1, z:z + 1]], axis=0)

    half_sweep(rows, at, explicit, g_ref, r_ref, gp_ref, last_ref, fwd_ref, out)
    last_g, last_r, gp = last_ref[0, at], last_ref[1, at], gp_ref[rows - 1, at]
    put_rows(out, 2, ends_ref[1, at] + last_r * gp * gp)
    put_rows(out, 3, last_g * gp)
    put_rows(out, 4, last_g * ends_ref[0, at])


def first_forward_kernel(
    rows, slab, cols, nx, nax,
    own_lo, own_hi, s_ref, g_ref, r_ref, gp_ref, part_ref, ends_ref, from_lo, from_hi, above_ref,
    last_ref, flux_ref, fwd_ref, send_ref, border_ref, own_border_ref,
    border_ports, lines,
):
    ix, ia = lax.axis_index("xs"), lax.axis_index("ax")
    above = jnp.where(ia < nax - 1, RZ, 0.0)
    c = above * s_ref[rows - 1] * above_ref[...]
    last_r = inverse(ends_ref[0] + c)
    last_ref[0] = c * last_r
    last_ref[1] = last_r

    for side, (own, halo, exists) in enumerate(((own_lo, from_lo, ix > 0), (own_hi, from_hi, ix < nx - 1))):
        s_own, state_own = own[0], own[1]
        s = jnp.where(exists, halo[0], 0.0)
        flux = SECTION_RATE * s_own * s * (halo[1] - state_own)
        lines[side, 0] = s
        lines[side, 1] = halo[2] - flux
        lines[side, 2] = RZ * s * pltpu.roll(s, rows - 1, 0)
        flux_ref[side] = flux

    row = lax.broadcasted_iota(jnp.int32, (8, cols), 0)

    def border(k, z):
        return jnp.where(row == 7, lines[0, k, z:z + 1], lines[1, k, z:z + 1])

    for z in range(rows):
        sb, eb = border(0, z), border(1, z)
        if z == 0:
            mb = gpb = jnp.ones_like(sb)
            first = sb
        else:
            eb = eb + gb * fb
            mb = 1.0 + gb * mb
            gpb = gpb * gb
        if z < rows - 1:
            cb = border(2, z)
            rb = inverse(mb + cb)
            gb = cb * rb
        else:
            rb = inverse(mb)
            gb = jnp.zeros_like(rb)
        fb = eb
        grb = gpb * rb
        ab = grb * gpb if z == 0 else ab + grb * gpb
        pb = grb * eb if z == 0 else pb + grb * eb
        for k, value in enumerate((sb, gb, rb, gpb, fb)):
            border_ref[k, z] = value
    zero = jnp.zeros_like(sb)
    for k, value in enumerate((ab, grb, rb, pb, rb * fb, first, sb, zero)):
        border_ports[0, k:k + 1] = value[7:8]
        border_ports[1, k:k + 1] = value[0:1]
    half = place()[3]
    first_half_sweep(rows, slab, cols, 1 - half, g_ref, r_ref, gp_ref, part_ref, ends_ref, flux_ref, last_ref, fwd_ref,
                     send_ref)
    send_ref[2 * PLANES] = border_ports[1 - half]
    own_border_ref[...] = border_ports[half]


def first_own_kernel(
    rows, slab, cols,
    g_ref, r_ref, gp_ref, part_ref, ends_ref, flux_ref, last_ref, own_border_ref,
    fwd_ref, mine_ref,
):
    first_half_sweep(rows, slab, cols, place()[3], g_ref, r_ref, gp_ref, part_ref, ends_ref, flux_ref, last_ref, fwd_ref,
                     mine_ref)
    mine_ref[2 * PLANES] = own_border_ref[...]


def place():
    i = lax.axis_index("ax")
    core, z, y = lax.rem(i, 2), lax.rem(lax.div(i, 2), 4), lax.div(i, 8)
    return core, z, y, lax.rem(core + z + y, 2)


def pick(index, options):
    value = options[0]
    for k in range(1, len(options)):
        value = jnp.where(index == k, options[k], value)
    return value


def ordered(index, mine, received):
    options = [mine] + [received[ORDER.index(step)] for step in range(1, 1 + len(received))] if len(received) > 1 else [mine, *received]
    return [pick(index ^ j, options) for j in range(1 + len(received))]


def main_planes(stack, planes):
    return [stack[2 * k:2 * k + 2] for k in planes]


def put(stack, at, value):
    stack[2 * at:2 * at + 2] = value


def join_coefs(low, high, lev, at):
    (alpha1, beta1, kappa1), (alpha2, beta2, kappa2) = low, high
    rho = inverse(1.0 + kappa1 * alpha2)
    x, y = beta1 * rho, beta2 * rho
    ax, ky = alpha2 * x, kappa1 * y
    for k, value in enumerate((rho, kappa1, alpha2, beta1, beta2, x, y, ax, ky)):
        put(lev, at * JOIN_COEFS + k, value)
    return alpha1 + beta1 * ax, x * beta2, kappa2 + beta2 * ky


def join_rhs(low, high, lev, at, values):
    (a1, b1), (a2, b2) = low, high
    rho, kappa1, alpha2, beta1, beta2 = main_planes(lev, range(at * JOIN_COEFS, at * JOIN_COEFS + 5))
    u0 = rho * (a2 + alpha2 * b1)
    q0 = rho * (b1 - kappa1 * a2)
    put(values, 2 * at, u0)
    put(values, 2 * at + 1, q0)
    return a1 + beta1 * u0, b2 + beta2 * q0


def join_border(low, high, lev, at):
    (a1, b1, d1, first1, last1, s_first, s1), (a2, b2, d2, first2, last2, s2, s_last) = low, high
    c = RZ * s1 * s2
    k = c * inverse(1.0 + c * (a2 + d1))
    f, k1, k2 = k * (first2 - last1), k * b1, k * b2
    for j, value in enumerate((f, k1, k2)):
        lev[at, j:j + 1] = value
    return a1 - k1 * b1, k1 * b2, d2 - k2 * b2, first1 + b1 * f, last2 - b2 * f, s_first, s_last


def join_all(groups, join):
    if len(groups) == 2:
        return join(groups[0], groups[1], 0)
    return join(join(groups[0], groups[1], 0), join(groups[2], groups[3], 1), 2)


def stage_coefs(index, mine, received, lev):
    stacks = [main_planes(stack, (2, 3, 4)) for stack in (mine, *received)]
    planes = [ordered(index, own[0], list(own[1:])) for own in zip(*stacks)]
    return join_all(list(zip(*planes)), lambda low, high, at: join_coefs(low, high, lev, at))


def stage_rhs(index, mine, received, lev, values):
    stacks = [main_planes(stack, (0, 1)) for stack in (mine, *received)]
    planes = [ordered(index, own[0], list(own[1:])) for own in zip(*stacks)]
    return join_all(list(zip(*planes)), lambda low, high, at: join_rhs(low, high, lev, at, values))


def stage_border(index, mine, received, lev):
    tiles = ordered(index, mine[2 * PLANES], [stack[2 * PLANES] for stack in received])
    groups = [[tile[k:k + 1] for k in range(7)] for tile in tiles]
    return join_all(groups, lambda low, high, at: join_border(low, high, lev, at))


def stage_index(stage):
    return place()[stage]


def first_join_kernel(stage, count, mine, *refs):
    received, (out, lev, values, border_lev) = refs[:count], refs[count:]
    index = stage_index(stage)
    for k, value in zip((2, 3, 4), stage_coefs(index, mine, received, lev)):
        put(out, k, value)
    for k, value in zip((0, 1), stage_rhs(index, mine, received, lev, values)):
        put(out, k, value)
    for k, value in enumerate(stage_border(index, mine, received, border_lev)):
        out[2 * PLANES, k:k + 1] = value
    out[2 * PLANES, 7:8] = jnp.zeros_like(value)


def second_join_kernel(stage, count, mine, *refs):
    received, (lev, out, values) = refs[:count], refs[count:]
    for k, value in zip((0, 1), stage_rhs(stage_index(stage), mine, received, lev, values)):
        put(out, k, value)


def choose(which, ats, stack, width, k):
    return pick(which, [stack[2 * (j * width + k):2 * (j * width + k) + 2] for j in ats])


def inside(lev, values, which, ats, q, top):
    u0, q0 = [choose(which, ats, values, 2, k) for k in (0, 1)]
    if q is None:
        return u0, q0
    x, y, ax, ky = [choose(which, ats, lev, JOIN_COEFS, k) for k in (5, 6, 7, 8)]
    return u0 + y * top + ax * q, q0 + x * q - ky * top


def descend(levs, values, mine_out, send_out):
    core, z, y, _ = place()
    q = top = None
    for stage, index in ((2, y), (1, z)):
        lev, value = levs[stage], values[stage]
        mid_top, mid_q = inside(lev, value, 0, (2,), q, top)
        if q is None:
            q = top = jnp.zeros_like(mid_q)
        high = index >= 2
        q, top = jnp.where(high, mid_q, q), jnp.where(high, top, mid_top)
        mid_top, mid_q = inside(lev, value, lax.div(index, 2), (0, 1), q, top)
        odd = lax.rem(index, 2) == 1
        q, top = jnp.where(odd, mid_q, q), jnp.where(odd, top, mid_top)
    mid_top, mid_q = inside(levs[0], values[0], 0, (0,), q, top)
    upper = core == 1
    put(mine_out, 0, jnp.where(upper, mid_q, q))
    put(mine_out, 1, jnp.where(upper, top, mid_top))
    put(send_out, 0, jnp.where(upper, q, mid_q))
    put(send_out, 1, jnp.where(upper, mid_top, top))


def descend_border(levs, mine_out, send_out):
    core, z, y, _ = place()
    lo = hi = jnp.zeros_like(mine_out[4, 0:1])

    def flux(lev, which, ats):
        f, k1, k2 = [pick(which, [lev[j, k:k + 1] for j in ats]) for k in range(3)]
        return f + k2 * hi - k1 * lo

    for stage, index in ((2, y), (1, z)):
        f = flux(levs[stage], 0, (2,))
        high = index >= 2
        lo, hi = jnp.where(high, -f, lo), jnp.where(high, hi, f)
        f = flux(levs[stage], lax.div(index, 2), (0, 1))
        odd = lax.rem(index, 2) == 1
        lo, hi = jnp.where(odd, -f, lo), jnp.where(odd, hi, f)
    f = flux(levs[0], 0, (0,))
    upper = core == 1
    mine_out[4], send_out[4] = jnp.zeros_like(mine_out[4]), jnp.zeros_like(send_out[4])
    mine_out[4, 0:1], mine_out[4, 1:2] = jnp.where(upper, -f, lo), jnp.where(upper, hi, f)
    send_out[4, 0:1], send_out[4, 1:2] = jnp.where(upper, lo, -f), jnp.where(upper, f, hi)


def first_last_kernel(count, mine, *refs):
    received = refs[:count]
    lev0, lev1, val0, val1, blev0, blev1, mine_out, send_out, lev2, val2, blev2 = refs[count:]
    index = stage_index(2)
    stage_coefs(index, mine, received, lev2)
    stage_rhs(index, mine, received, lev2, val2)
    stage_border(index, mine, received, blev2)
    descend((lev0, lev1, lev2), (val0, val1, val2), mine_out, send_out)
    descend_border((blev0, blev1, blev2), mine_out, send_out)


def second_last_kernel(count, mine, *refs):
    received = refs[:count]
    lev0, lev1, lev2, val0, val1, mine_out, send_out, val2 = refs[count:]
    stage_rhs(stage_index(2), mine, received, lev2, val2)
    descend((lev0, lev1, lev2), (val0, val1, val2), mine_out, send_out)


def half_state(rows, at, ports, g_ref, r_ref, gp_ref, fwd_ref, last_ref, keep_ref, source_ref, emit):
    q = jnp.concatenate([ports[0], ports[1]], axis=0)
    u = jnp.concatenate([ports[2], ports[3]], axis=0)
    for z in range(rows - 1, -1, -1):
        r = r_ref[z, at] if z < rows - 1 else last_ref[1, at]
        g = g_ref[z, at] if z < rows - 1 else last_ref[0, at]
        u = r * (fwd_ref[z] + gp_ref[z, at] * q) + g * u
        emit(z, source_ref[z, at] + keep_ref[z, at] * u)


def own_state_kernel(rows, slab, own, g_ref, r_ref, gp_ref, fwd_ref, last_ref, keep_ref, source_ref, state_ref):
    def emit(z, state):
        state_ref[z] = state

    half_state(rows, half_rows(slab, place()[3]), own, g_ref, r_ref, gp_ref, fwd_ref, last_ref, keep_ref, source_ref, emit)


def split_cols(tile):
    return [tile[:, c:c + 128] for c in range(0, tile.shape[-1], 128)]


def half_tiles(plane):
    return [split_cols(plane[t:t + 8]) for t in range(0, plane.shape[0], 8)]


def products(left, right):
    return [[x * y for x, y in zip(*lines)] for lines in zip(left, right)]


def put_tiles(ref, z, tiles):
    for t, line in enumerate(tiles):
        for c, tile in enumerate(line):
            ref[z, 8 * t:8 * t + 8, 128 * c:128 * c + 128] = tile


def explicit_tiles(state, s, vsum, ssum):
    return [[x + SECTION_RATE * w * (v - x * n) for x, w, v, n in zip(*lines)] for lines in zip(state, s, vsum, ssum)]


def own_explicit_kernel(
    rows, slab,
    own, s_ref, g_ref, r_ref, gp_ref, fwd_ref, last_ref, keep_ref, source_ref, ssum_ref,
    state_ref, part_ref,
):
    at = half_rows(slab, place()[3])

    def emit(z, state):
        state_ref[z] = state
        state, s = half_tiles(state), half_tiles(s_ref[z, at])
        put_tiles(part_ref, z, explicit_tiles(state, s, neighbour_sum(products(s, state)), half_tiles(ssum_ref[z, at])))

    half_state(rows, at, own, g_ref, r_ref, gp_ref, fwd_ref, last_ref, keep_ref, source_ref, emit)


def middle_kernel(
    rows, slab, cols,
    own, other, state_own, part_own, s_ref, g_ref, r_ref, gp_ref, fwd_in, last_ref, keep_ref, source_ref, ssum_ref,
    border_ref, reaction_lo, reaction_hi,
    e_own, fwd_ref, send_ref,
    e_other,
):
    row = lax.broadcasted_iota(jnp.int32, (8, cols), 0)
    half = place()[3]
    second = half == 1
    low_tile, high_tile = jnp.where(second, other[4], own[4]), jnp.where(second, own[4], other[4])
    inflow_b = jnp.where(row == 7, low_tile[0:1], high_tile[0:1])
    border = [jnp.where(row == 7, low_tile[1:2], high_tile[1:2])]
    narrow = lax.broadcasted_iota(jnp.int32, (8, 128), 0)
    bottom = narrow == 7
    mine, at = half_rows(slab, half), half_rows(slab, 1 - half)

    def around(is_second, flow_b, neighbour):
        return [jnp.where(is_second, jnp.where(bottom, high, b), jnp.where(bottom, b, low))
                for b, low, high in zip(flow_b, neighbour[0], neighbour[1])]

    def border_part(is_second, tile):
        return [jnp.where(is_second, jnp.where(bottom, 0.0, x), jnp.where(bottom, x, 0.0)) for x in tile]

    def to_rows(tile):
        return ([jnp.where(narrow == 0, pltpu.roll(x, 1, 0), 0.0) for x in tile],
                [jnp.where(narrow == 7, pltpu.roll(x, 7, 0), 0.0) for x in tile])

    def explicit(z, new):
        sb, gb, rb, gpb, fb = [border_ref[k, z] for k in range(5)]
        keep_b, source_b = [jnp.where(row == 7, reaction_lo[k, z:z + 1], reaction_hi[k, z:z + 1]) for k in (0, 1)]
        rhs = fb + gpb * inflow_b
        ub = border[0] = rb * (rhs + border[0]) if z == rows - 1 else rb * rhs + gb * border[0]
        flow_b = split_cols(sb * (source_b + keep_b * ub))
        sb = split_cols(sb)
        kept, s_kept = half_tiles(state_own[z]), half_tiles(s_ref[z, mine])
        state, s = half_tiles(new), half_tiles(s_ref[z, at])
        flow_kept, flow = products(s_kept, kept), products(s, state)

        ssum = half_tiles(ssum_ref[z, at])
        ssum = [[x + y for x, y in zip(*lines)] for lines in zip(ssum, to_rows(border_part(half == 0, sb)))]
        vsum = neighbour_sum(flow, around(half == 0, flow_b, flow_kept))
        put_tiles(e_other, z, explicit_tiles(state, s, vsum, ssum))

        v_more, s_more = to_rows(around(second, flow_b, flow)), to_rows(border_part(second, sb))
        part = half_tiles(part_own[z])
        put_tiles(e_own, z, [
            [p + SECTION_RATE * w * (v - x * n) for p, w, v, x, n in zip(*lines)]
            for lines in zip(part, s_kept, v_more, kept, s_more)])

    half_state(rows, at, other, g_ref, r_ref, gp_ref, fwd_in, last_ref, keep_ref, source_ref, explicit)
    half_sweep(rows, at, lambda z: e_other[z], g_ref, r_ref, gp_ref, last_ref, fwd_ref, send_ref)


def second_own_kernel(rows, slab, e_ref, g_ref, r_ref, gp_ref, last_ref, fwd_ref, mine_ref):
    at = half_rows(slab, place()[3])
    half_sweep(rows, at, lambda z: e_ref[z], g_ref, r_ref, gp_ref, last_ref, fwd_ref, mine_ref)


def final_kernel(
    rows, slab,
    other, state_own, g_ref, r_ref, gp_ref, fwd_ref, last_ref, keep_ref, source_ref,
    out_hbm, out, sems, own_sem,
):
    half = place()[3]
    own_copy = pltpu.make_async_copy(state_own, out_hbm.at[:, half_rows(slab, half)], own_sem)
    own_copy.start()
    at = half_rows(slab, 1 - half)
    copies = []

    def emit(z, state):
        out[z] = state
        if z % CHUNK == 0:
            here = pl.ds(z, CHUNK)
            copy = pltpu.make_async_copy(out.at[here], out_hbm.at[here, at], sems.at[z // CHUNK])
            copy.start()
            copies.append(copy)

    half_state(rows, at, other, g_ref, r_ref, gp_ref, fwd_ref, last_ref, keep_ref, source_ref, emit)
    for copy in copies:
        copy.wait()
    own_copy.wait()


def on_device(partners, concentration, tissue_mask, wall_layer, stiffness, production, layer_diffusivity, uptake_rate):
    rows, slab, cols = concentration.shape
    nx, nax = lax.axis_size("xs"), lax.axis_size("ax")
    block = (rows, slab, cols)
    smem = pl.BlockSpec(memory_space=pltpu.SMEM)
    hbm = pl.BlockSpec(memory_space=pltpu.HBM)

    def in_hbm(x):
        return pltpu.with_memory_space_constraint(x, pltpu.HBM)

    def call(kernel, outs, operands, scratch=(), specs=None, out_specs=None, us=1.0):
        return pl.pallas_call(
            kernel,
            out_shape=outs,
            in_specs=specs or [vspec()] * len(operands),
            out_specs=out_specs or [vspec()] * len(outs),
            scratch_shapes=list(scratch),
            compiler_params=params(),
            cost_estimate=cost(us),
        )(*operands)

    def exchange(block, stage):
        received = {step: lax.ppermute(block, "ax", route) for step, route in partners[stage]}
        return [received[step] for step, _ in partners[stage]]

    def f32(*shape):
        return pltpu.VMEM(shape, jnp.float32)

    def i32(*shape):
        return pltpu.VMEM(shape, jnp.int32)

    conc, mask, layer, stiff = [
        in_hbm(x) for x in (concentration, tissue_mask, wall_layer, stiffness)]
    diff_table, uptake_rate = in_hbm(layer_diffusivity), in_hbm(uptake_rate)
    lo, hi, first_s = call(
        functools.partial(edge_kernel, slab, cols),
        [at_vmem(3, rows, cols), at_vmem(3, rows, cols), at_vmem(slab, cols)],
        [diff_table, conc, mask, layer, stiff],
        scratch=[i32(2, 2, rows, cols), i32(2, 2, rows, cols), f32(2, 4, rows, cols),
                 i32(slab, cols), i32(slab, cols), f32(slab, cols),
                 pltpu.SemaphoreType.DMA((2, 8)), pltpu.SemaphoreType.DMA((3,))],
        specs=[smem] + [hbm] * 4,
    )
    def from_neighbours(lo, hi):
        return (lax.ppermute(hi, "xs", [(i, (i + 1) % nx) for i in range(nx)]),
                lax.ppermute(lo, "xs", [((i + 1) % nx, i) for i in range(nx)]))

    from_lo, from_hi = from_neighbours(lo, hi)
    above_s = lax.ppermute(first_s, "ax", [((i + 1) % nax, i) for i in range(nax)])

    s, g, r, gp, ssum, part, ends = call(
        functools.partial(setup_kernel, rows, slab, cols),
        [at_vmem(*block)] * 6 + [at_vmem(2, slab, cols)],
        [diff_table, concentration, tissue_mask, wall_layer, stiffness],
        specs=[smem] + [vspec()] * 4,
        us=5.0,
    )
    stack, pair = 2 * PLANES + 1, (5, 8, cols)
    half_block = (rows, slab // 2, cols)
    last, flux, fwd_other, send, border, own_border = call(
        functools.partial(first_forward_kernel, rows, slab, cols, nx, nax),
        [at_vmem(2, slab, cols), at_vmem(2, rows, cols), at_vmem(*half_block), at_vmem(stack, 8, cols),
         at_vmem(5, rows, 8, cols), at_vmem(8, cols)],
        [lo, hi, s, g, r, gp, part, ends, from_lo, from_hi, above_s],
        scratch=[f32(2, 8, cols), f32(2, 3, rows, cols)],
    )
    fwd_own, mine = call(
        functools.partial(first_own_kernel, rows, slab, cols),
        [at_vmem(*half_block), at_vmem(stack, 8, cols)],
        [g, r, gp, part, ends, flux, last, own_border],
    )

    levs, values, border_levs = [], [], []
    for stage in (0, 1):
        received = exchange(mine if stage else send, stage)
        joins = len(received)
        if stage == 1:
            uptake_late, mine = lax.optimization_barrier((uptake_rate, mine))
            keep, source, lo, hi = call(
                functools.partial(reaction_kernel, rows),
                [at_vmem(*block)] * 2 + [at_vmem(2, rows, cols)] * 2,
                [uptake_late, tissue_mask, wall_layer, production],
                specs=[smem] + [vspec()] * 3,
                us=2.0,
            )
            reaction_lo, reaction_hi = from_neighbours(lo, hi)
            mine, keep, source = lax.optimization_barrier((mine, keep, source))
        mine, lev, value, border_lev = call(
            functools.partial(first_join_kernel, stage, joins),
            [at_vmem(stack, 8, cols), at_vmem(2 * JOIN_COEFS * joins, 8, cols), at_vmem(4 * joins, 8, cols),
             at_vmem(joins, 8, cols)],
            [mine, *received],
        )
        levs.append(lev)
        values.append(value)
        border_levs.append(border_lev)
    received = exchange(mine, 2)
    joins = len(received)
    own, send, lev = call(
        functools.partial(first_last_kernel, joins),
        [at_vmem(*pair), at_vmem(*pair), at_vmem(2 * JOIN_COEFS * joins, 8, cols)],
        [mine, *received, *levs, *values, *border_levs],
        scratch=[f32(4 * joins, 8, cols), f32(joins, 8, cols)],
    )
    levs.append(lev)
    (other,) = exchange(send, 0)
    state_own, part_own = call(
        functools.partial(own_explicit_kernel, rows, slab),
        [at_vmem(*half_block)] * 2,
        [own, s, g, r, gp, fwd_own, last, keep, source, ssum],
    )
    e, fwd_other, send = call(
        functools.partial(middle_kernel, rows, slab, cols),
        [at_vmem(*half_block), at_vmem(*half_block), at_vmem(4, 8, cols)],
        [own, other, state_own, part_own, s, g, r, gp, fwd_other, last, keep, source, ssum, border,
         reaction_lo, reaction_hi],
        scratch=[f32(*half_block)],
        us=3.0,
    )
    fwd_own, mine = call(
        functools.partial(second_own_kernel, rows, slab),
        [at_vmem(*half_block), at_vmem(4, 8, cols)],
        [e, g, r, gp, last],
    )
    values = []
    for stage in (0, 1):
        received = exchange(mine if stage else send, stage)
        joins = len(received)
        mine, value = call(
            functools.partial(second_join_kernel, stage, joins),
            [at_vmem(4, 8, cols), at_vmem(4 * joins, 8, cols)],
            [mine, *received, levs[stage]],
        )
        values.append(value)
    received = exchange(mine, 2)
    joins = len(received)
    own, send = call(
        functools.partial(second_last_kernel, joins),
        [at_vmem(4, 8, cols), at_vmem(4, 8, cols)],
        [mine, *received, *levs, *values],
        scratch=[f32(4 * joins, 8, cols)],
    )
    (other,) = exchange(send, 0)
    (state_own,) = call(
        functools.partial(own_state_kernel, rows, slab),
        [at_vmem(*half_block)],
        [own, g, r, gp, fwd_own, last, keep, source],
    )
    (out,) = call(
        functools.partial(final_kernel, rows, slab),
        [jax.ShapeDtypeStruct(block, jnp.float32)],
        [other, state_own, g, r, gp, fwd_other, last, keep, source],
        scratch=[f32(*half_block), pltpu.SemaphoreType.DMA((rows // CHUNK,)), pltpu.SemaphoreType.DMA],
        out_specs=[hbm],
    )
    return out


def join_partners():
    stages = (
        ((1, lambda y, z, c: (y, z, 1 - c)),),
        tuple((k, lambda y, z, c, k=k: (y, z ^ k, c ^ (k & 1))) for k in ORDER),
        tuple((k, lambda y, z, c, k=k: (y ^ k, z, c ^ (k & 1))) for k in ORDER),
    )
    routes = []
    for flips in stages:
        routes.append([])
        for step, flip in flips:
            route = []
            for i in range(32):
                y, z, c = flip(i // 8, i // 2 % 4, i % 2)
                route.append((i, y * 8 + z * 2 + c))
            routes[-1].append((step, route))
    return routes


def solution(mesh):
    placed = (P("ax", "xs", None),) * 5 + (P(), P())
    return jax.shard_map(
        functools.partial(on_device, join_partners()),
        mesh=mesh, in_specs=placed, out_specs=P("ax", "xs", None), check_vma=False,
    )
```

```python
import functools

import jax
import jax.numpy as jnp
from jax import lax
from jax.experimental import pallas as pl
from jax.experimental.pallas import tpu as pltpu
from jax.sharding import PartitionSpec as P

RZ = 3072.0
SECTION_RATE = 0.05
LAYERS = 4
LIMIT = 24 * 1024 * 1024
CHUNK = 8
PLANES = 5
JOIN_COEFS = 9
ORDER = (1, 3, 2)


def at_vmem(*shape):
    return pltpu.VMEM(shape, jnp.float32)


def vspec():
    return pl.BlockSpec(memory_space=pltpu.VMEM)


def params():
    return pltpu.CompilerParams(vmem_limit_bytes=LIMIT)


def cost(us):
    return pl.CostEstimate(flops=int(us * 2e6), bytes_accessed=int(us * 3e6), transcendentals=0)


def lookup(labels, table):
    value = table[LAYERS - 1]
    for layer in range(LAYERS - 1):
        value = jnp.where(labels == layer, table[layer], value)
    return value


def root_diffusivity(mask, layer, stiff, table):
    inside = lookup(layer, table) * stiff
    return jnp.where(mask == 0, 0.0, inside * lax.rsqrt(inside))


def inverse(x):
    return pl.reciprocal(x, approx=True)


def tiles_of(ref, z, slab, cols):
    return [[ref[z, t:t + 8, c:c + 128] for c in range(0, cols, 128)] for t in range(0, slab, 8)]


def neighbour_sum(tiles, border=None):
    rows, cols = len(tiles), len(tiles[0])
    row = lax.broadcasted_iota(jnp.int32, (8, 128), 0)
    lane = lax.broadcasted_iota(jnp.int32, (8, 128), 1)

    def rolled(shift, axis):
        return [[pltpu.roll(tile, shift, axis) for tile in line] for line in tiles]

    down, up, right, left = rolled(1, 0), rolled(7, 0), rolled(1, 1), rolled(127, 1)
    if border is not None:
        down.append([pltpu.roll(tile, 1, 0) for tile in border])
        up.append([pltpu.roll(tile, 7, 0) for tile in border])

    def at(array, t, c):
        if 0 <= c < cols and 0 <= t < rows:
            return array[t][c]
        return 0.0 if border is None or not 0 <= c < cols else array[rows][c]

    return [[
        (jnp.where(row == 0, at(down, t - 1, c), down[t][c]) + jnp.where(row == 7, at(up, t + 1, c), up[t][c]))
        + (jnp.where(lane == 0, at(right, t, c - 1), right[t][c])
           + jnp.where(lane == 127, at(left, t, c + 1), left[t][c]))
        for c in range(cols)] for t in range(rows)]


def along_cols(plane):
    cols = plane.shape[-1]
    lane = lax.broadcasted_iota(jnp.int32, plane.shape, 1)
    return (jnp.where(lane == 0, 0.0, pltpu.roll(plane, 1, 1))
            + jnp.where(lane == cols - 1, 0.0, pltpu.roll(plane, cols - 1, 1)))


def read_table(table):
    return [table[k] for k in range(LAYERS)]


def edge_kernel(
    slab, cols,
    diff_table, conc_hbm, mask_hbm, layer_hbm, stiff_hbm,
    lo_out, hi_out, first_out,
    mask, layer, floats, mask_row, layer_row, stiff_row, sems, row_sems,
):
    copies = []
    for side in (0, 1):
        sources = []
        for depth in (0, 1):
            x = depth if side == 0 else slab - 1 - depth
            sources += [(mask_hbm.at[:, x], mask.at[side, depth]), (layer_hbm.at[:, x], layer.at[side, depth]),
                        (stiff_hbm.at[:, x], floats.at[side, depth]), (conc_hbm.at[:, x], floats.at[side, 2 + depth])]
        copies.append([
            pltpu.make_async_copy(source, target, sems.at[side, k]) for k, (source, target) in enumerate(sources)])
    copies.append([
        pltpu.make_async_copy(source.at[0], target, row_sems.at[k])
        for k, (source, target) in enumerate(((mask_hbm, mask_row), (layer_hbm, layer_row), (stiff_hbm, stiff_row)))])
    for group in copies:
        for copy in group:
            copy.start(priority=1)
    table = read_table(diff_table)
    for side, out in ((0, lo_out), (1, hi_out)):
        for copy in copies[side]:
            copy.wait()
        s, inner = [root_diffusivity(mask[side, d], layer[side, d], floats[side, d], table) for d in (0, 1)]
        state = floats[side, 2]
        ssum = inner + along_cols(s)
        vsum = inner * floats[side, 3] + along_cols(s * state)
        out[0] = s
        out[1] = state
        out[2] = state + SECTION_RATE * s * (vsum - state * ssum)
    for copy in copies[2]:
        copy.wait()
    first_out[...] = root_diffusivity(mask_row[...], layer_row[...], stiff_row[...], table)


def setup_kernel(
    rows, slab, cols,
    table, conc, mask, layer, stiff,
    s_out, g_out, r_out, gp_out, ssum_out, part_out, ends_out,
):
    weights = read_table(table)
    grid = [(t, c) for t in range(slab // 8) for c in range(cols // 128)]
    s = m = gp = alpha = None
    for z in range(rows):
        w, lab, sti, st = [tiles_of(ref, z, slab, cols) for ref in (mask, layer, stiff, conc)]
        s_next = [[root_diffusivity(w[t][c], lab[t][c], sti[t][c], weights)
                   for c in range(cols // 128)] for t in range(slab // 8)]
        flow = [[s_next[t][c] * st[t][c] for c in range(cols // 128)] for t in range(slab // 8)]
        ssum, vsum = neighbour_sum(s_next), neighbour_sum(flow)
        for t, c in grid:
            here = (z, pl.ds(8 * t, 8), pl.ds(128 * c, 128))
            s_out[here] = s_next[t][c]
            ssum_out[here] = ssum[t][c]
            part_out[here] = st[t][c] + SECTION_RATE * s_next[t][c] * (vsum[t][c] - st[t][c] * ssum[t][c])
        if z == 0:
            ones = {k: jnp.ones((8, 128), jnp.float32) for k in grid}
            m, gp, alpha = dict(ones), dict(ones), {k: jnp.zeros((8, 128), jnp.float32) for k in grid}
        else:
            for t, c in grid:
                k = (t, c)
                here = (z - 1, pl.ds(8 * t, 8), pl.ds(128 * c, 128))
                couple = RZ * s[t][c] * s_next[t][c]
                r = inverse(m[k] + couple)
                g = couple * r
                r_out[here] = r
                g_out[here] = g
                gp_out[here] = gp[k]
                alpha[k] = alpha[k] + r * (gp[k] * gp[k])
                m[k] = 1.0 + g * m[k]
                gp[k] = gp[k] * g
        s = s_next
    for t, c in grid:
        here = (pl.ds(8 * t, 8), pl.ds(128 * c, 128))
        gp_out[(rows - 1,) + here] = gp[t, c]
        ends_out[(0,) + here] = m[t, c]
        ends_out[(1,) + here] = alpha[t, c]


def reaction_kernel(rows, uptake_table, mask, layer, prod, keep_out, source_out, lo_out, hi_out):
    tab = read_table(uptake_table)
    for z in range(rows):
        weight = mask[z].astype(jnp.float32)
        keep = 1.0 - weight * lookup(layer[z], tab)
        source = weight * prod[z]
        keep_out[z] = keep
        source_out[z] = source
        lo_out[0, z:z + 1] = keep[0:1]
        lo_out[1, z:z + 1] = source[0:1]
        hi_out[0, z:z + 1] = keep[-1:]
        hi_out[1, z:z + 1] = source[-1:]


def tile_of(tiles, k):
    return tiles[8 * k:8 * k + 8]


def half_rows(slab, which):
    return pl.ds(pl.multiple_of(which * (slab // 2), slab // 2), slab // 2)


def put_rows(stack, k, value):
    stack[2 * k], stack[2 * k + 1] = value[:8], value[8:]


def half_sweep(rows, at, explicit, g_ref, r_ref, gp_ref, last_ref, fwd_ref, out):
    total = e = None
    for z in range(rows):
        e = explicit(z) if z == 0 else explicit(z) + g_ref[z - 1, at] * e
        fwd_ref[z] = e
        term = gp_ref[z, at] * (r_ref[z, at] if z < rows - 1 else last_ref[1, at]) * e
        total = term if z == 0 else total + term
    put_rows(out, 0, total)
    put_rows(out, 1, last_ref[0, at] * e)


def first_half_sweep(rows, slab, cols, which, g_ref, r_ref, gp_ref, part_ref, ends_ref, flux_ref, last_ref, fwd_ref, out):
    at = half_rows(slab, which)
    row = lax.broadcasted_iota(jnp.int32, (8, cols), 0)
    lo = jnp.where(row == jnp.where(which == 0, 0, -1), 1.0, 0.0)
    hi = jnp.where(row == jnp.where(which == 1, 7, -1), 1.0, 0.0)

    def explicit(z):
        part = part_ref[z, at]
        return jnp.concatenate(
            [part[:8] + lo * flux_ref[0, z:z + 1], part[8:] + hi * flux_ref[1, z:z + 1]], axis=0)

    half_sweep(rows, at, explicit, g_ref, r_ref, gp_ref, last_ref, fwd_ref, out)
    last_g, last_r, gp = last_ref[0, at], last_ref[1, at], gp_ref[rows - 1, at]
    put_rows(out, 2, ends_ref[1, at] + last_r * gp * gp)
    put_rows(out, 3, last_g * gp)
    put_rows(out, 4, last_g * ends_ref[0, at])


def first_forward_kernel(
    rows, slab, cols, nx, nax,
    own_lo, own_hi, s_ref, g_ref, r_ref, gp_ref, part_ref, ends_ref, from_lo, from_hi, above_ref,
    last_ref, flux_ref, fwd_ref, send_ref, border_ref, own_border_ref,
    border_ports, lines,
):
    ix, ia = lax.axis_index("xs"), lax.axis_index("ax")
    above = jnp.where(ia < nax - 1, RZ, 0.0)
    c = above * s_ref[rows - 1] * above_ref[...]
    last_r = inverse(ends_ref[0] + c)
    last_ref[0] = c * last_r
    last_ref[1] = last_r

    for side, (own, halo, exists) in enumerate(((own_lo, from_lo, ix > 0), (own_hi, from_hi, ix < nx - 1))):
        s_own, state_own = own[0], own[1]
        s = jnp.where(exists, halo[0], 0.0)
        flux = SECTION_RATE * s_own * s * (halo[1] - state_own)
        lines[side, 0] = s
        lines[side, 1] = halo[2] - flux
        lines[side, 2] = RZ * s * pltpu.roll(s, rows - 1, 0)
        flux_ref[side] = flux

    row = lax.broadcasted_iota(jnp.int32, (8, cols), 0)

    def border(k, z):
        return jnp.where(row == 7, lines[0, k, z:z + 1], lines[1, k, z:z + 1])

    for z in range(rows):
        sb, eb = border(0, z), border(1, z)
        if z == 0:
            mb = gpb = jnp.ones_like(sb)
            first = sb
        else:
            eb = eb + gb * fb
            mb = 1.0 + gb * mb
            gpb = gpb * gb
        if z < rows - 1:
            cb = border(2, z)
            rb = inverse(mb + cb)
            gb = cb * rb
        else:
            rb = inverse(mb)
            gb = jnp.zeros_like(rb)
        fb = eb
        grb = gpb * rb
        ab = grb * gpb if z == 0 else ab + grb * gpb
        pb = grb * eb if z == 0 else pb + grb * eb
        for k, value in enumerate((sb, gb, rb, gpb, fb)):
            border_ref[k, z] = value
    zero = jnp.zeros_like(sb)
    for k, value in enumerate((ab, grb, rb, pb, rb * fb, first, sb, zero)):
        border_ports[0, k:k + 1] = value[7:8]
        border_ports[1, k:k + 1] = value[0:1]
    half = place()[3]
    first_half_sweep(rows, slab, cols, 1 - half, g_ref, r_ref, gp_ref, part_ref, ends_ref, flux_ref, last_ref, fwd_ref,
                     send_ref)
    send_ref[2 * PLANES] = border_ports[1 - half]
    own_border_ref[...] = border_ports[half]


def first_own_kernel(
    rows, slab, cols,
    g_ref, r_ref, gp_ref, part_ref, ends_ref, flux_ref, last_ref, own_border_ref,
    fwd_ref, mine_ref,
):
    first_half_sweep(rows, slab, cols, place()[3], g_ref, r_ref, gp_ref, part_ref, ends_ref, flux_ref, last_ref, fwd_ref,
                     mine_ref)
    mine_ref[2 * PLANES] = own_border_ref[...]


def place():
    i = lax.axis_index("ax")
    core, z, y = lax.rem(i, 2), lax.rem(lax.div(i, 2), 4), lax.div(i, 8)
    return core, z, y, lax.rem(core + z + y, 2)


def pick(index, options):
    value = options[0]
    for k in range(1, len(options)):
        value = jnp.where(index == k, options[k], value)
    return value


def ordered(index, mine, received):
    options = [mine] + [received[ORDER.index(step)] for step in range(1, 1 + len(received))] if len(received) > 1 else [mine, *received]
    return [pick(index ^ j, options) for j in range(1 + len(received))]


def main_planes(stack, planes):
    return [stack[2 * k:2 * k + 2] for k in planes]


def put(stack, at, value):
    stack[2 * at:2 * at + 2] = value


def join_coefs(low, high, lev, at):
    (alpha1, beta1, kappa1), (alpha2, beta2, kappa2) = low, high
    rho = inverse(1.0 + kappa1 * alpha2)
    x, y = beta1 * rho, beta2 * rho
    ax, ky = alpha2 * x, kappa1 * y
    for k, value in enumerate((rho, kappa1, alpha2, beta1, beta2, x, y, ax, ky)):
        put(lev, at * JOIN_COEFS + k, value)
    return alpha1 + beta1 * ax, x * beta2, kappa2 + beta2 * ky


def join_rhs(low, high, lev, at, values):
    (a1, b1), (a2, b2) = low, high
    rho, kappa1, alpha2, beta1, beta2 = main_planes(lev, range(at * JOIN_COEFS, at * JOIN_COEFS + 5))
    u0 = rho * (a2 + alpha2 * b1)
    q0 = rho * (b1 - kappa1 * a2)
    put(values, 2 * at, u0)
    put(values, 2 * at + 1, q0)
    return a1 + beta1 * u0, b2 + beta2 * q0


def join_border(low, high, lev, at):
    (a1, b1, d1, first1, last1, s_first, s1), (a2, b2, d2, first2, last2, s2, s_last) = low, high
    c = RZ * s1 * s2
    k = c * inverse(1.0 + c * (a2 + d1))
    f, k1, k2 = k * (first2 - last1), k * b1, k * b2
    for j, value in enumerate((f, k1, k2)):
        lev[at, j:j + 1] = value
    return a1 - k1 * b1, k1 * b2, d2 - k2 * b2, first1 + b1 * f, last2 - b2 * f, s_first, s_last


def join_all(groups, join):
    if len(groups) == 2:
        return join(groups[0], groups[1], 0)
    return join(join(groups[0], groups[1], 0), join(groups[2], groups[3], 1), 2)


def stage_coefs(index, mine, received, lev):
    stacks = [main_planes(stack, (2, 3, 4)) for stack in (mine, *received)]
    planes = [ordered(index, own[0], list(own[1:])) for own in zip(*stacks)]
    return join_all(list(zip(*planes)), lambda low, high, at: join_coefs(low, high, lev, at))


def stage_rhs(index, mine, received, lev, values):
    stacks = [main_planes(stack, (0, 1)) for stack in (mine, *received)]
    planes = [ordered(index, own[0], list(own[1:])) for own in zip(*stacks)]
    return join_all(list(zip(*planes)), lambda low, high, at: join_rhs(low, high, lev, at, values))


def stage_border(index, mine, received, lev):
    tiles = ordered(index, mine[2 * PLANES], [stack[2 * PLANES] for stack in received])
    groups = [[tile[k:k + 1] for k in range(7)] for tile in tiles]
    return join_all(groups, lambda low, high, at: join_border(low, high, lev, at))


def stage_index(stage):
    return place()[stage]


def first_join_kernel(stage, count, mine, *refs):
    received, (out, lev, values, border_lev) = refs[:count], refs[count:]
    index = stage_index(stage)
    for k, value in zip((2, 3, 4), stage_coefs(index, mine, received, lev)):
        put(out, k, value)
    for k, value in zip((0, 1), stage_rhs(index, mine, received, lev, values)):
        put(out, k, value)
    for k, value in enumerate(stage_border(index, mine, received, border_lev)):
        out[2 * PLANES, k:k + 1] = value
    out[2 * PLANES, 7:8] = jnp.zeros_like(value)


def second_join_kernel(stage, count, mine, *refs):
    received, (lev, out, values) = refs[:count], refs[count:]
    for k, value in zip((0, 1), stage_rhs(stage_index(stage), mine, received, lev, values)):
        put(out, k, value)


def choose(which, ats, stack, width, k):
    return pick(which, [stack[2 * (j * width + k):2 * (j * width + k) + 2] for j in ats])


def inside(lev, values, which, ats, q, top):
    u0, q0 = [choose(which, ats, values, 2, k) for k in (0, 1)]
    if q is None:
        return u0, q0
    x, y, ax, ky = [choose(which, ats, lev, JOIN_COEFS, k) for k in (5, 6, 7, 8)]
    return u0 + y * top + ax * q, q0 + x * q - ky * top


def descend(levs, values, mine_out, send_out):
    core, z, y, _ = place()
    q = top = None
    for stage, index in ((2, y), (1, z)):
        lev, value = levs[stage], values[stage]
        mid_top, mid_q = inside(lev, value, 0, (2,), q, top)
        if q is None:
            q = top = jnp.zeros_like(mid_q)
        high = index >= 2
        q, top = jnp.where(high, mid_q, q), jnp.where(high, top, mid_top)
        mid_top, mid_q = inside(lev, value, lax.div(index, 2), (0, 1), q, top)
        odd = lax.rem(index, 2) == 1
        q, top = jnp.where(odd, mid_q, q), jnp.where(odd, top, mid_top)
    mid_top, mid_q = inside(levs[0], values[0], 0, (0,), q, top)
    upper = core == 1
    put(mine_out, 0, jnp.where(upper, mid_q, q))
    put(mine_out, 1, jnp.where(upper, top, mid_top))
    put(send_out, 0, jnp.where(upper, q, mid_q))
    put(send_out, 1, jnp.where(upper, mid_top, top))


def descend_border(levs, mine_out, send_out):
    core, z, y, _ = place()
    lo = hi = jnp.zeros_like(mine_out[4, 0:1])

    def flux(lev, which, ats):
        f, k1, k2 = [pick(which, [lev[j, k:k + 1] for j in ats]) for k in range(3)]
        return f + k2 * hi - k1 * lo

    for stage, index in ((2, y), (1, z)):
        f = flux(levs[stage], 0, (2,))
        high = index >= 2
        lo, hi = jnp.where(high, -f, lo), jnp.where(high, hi, f)
        f = flux(levs[stage], lax.div(index, 2), (0, 1))
        odd = lax.rem(index, 2) == 1
        lo, hi = jnp.where(odd, -f, lo), jnp.where(odd, hi, f)
    f = flux(levs[0], 0, (0,))
    upper = core == 1
    mine_out[4], send_out[4] = jnp.zeros_like(mine_out[4]), jnp.zeros_like(send_out[4])
    mine_out[4, 0:1], mine_out[4, 1:2] = jnp.where(upper, -f, lo), jnp.where(upper, hi, f)
    send_out[4, 0:1], send_out[4, 1:2] = jnp.where(upper, lo, -f), jnp.where(upper, f, hi)


def first_last_kernel(count, mine, *refs):
    received = refs[:count]
    lev0, lev1, val0, val1, blev0, blev1, mine_out, send_out, lev2, val2, blev2 = refs[count:]
    index = stage_index(2)
    stage_coefs(index, mine, received, lev2)
    stage_rhs(index, mine, received, lev2, val2)
    stage_border(index, mine, received, blev2)
    descend((lev0, lev1, lev2), (val0, val1, val2), mine_out, send_out)
    descend_border((blev0, blev1, blev2), mine_out, send_out)


def second_last_kernel(count, mine, *refs):
    received = refs[:count]
    lev0, lev1, lev2, val0, val1, mine_out, send_out, val2 = refs[count:]
    stage_rhs(stage_index(2), mine, received, lev2, val2)
    descend((lev0, lev1, lev2), (val0, val1, val2), mine_out, send_out)


def half_state(rows, at, ports, g_ref, r_ref, gp_ref, fwd_ref, last_ref, keep_ref, source_ref, emit):
    q = jnp.concatenate([ports[0], ports[1]], axis=0)
    u = jnp.concatenate([ports[2], ports[3]], axis=0)
    for z in range(rows - 1, -1, -1):
        r = r_ref[z, at] if z < rows - 1 else last_ref[1, at]
        g = g_ref[z, at] if z < rows - 1 else last_ref[0, at]
        u = r * (fwd_ref[z] + gp_ref[z, at] * q) + g * u
        emit(z, source_ref[z, at] + keep_ref[z, at] * u)


def own_state_kernel(rows, slab, own, g_ref, r_ref, gp_ref, fwd_ref, last_ref, keep_ref, source_ref, state_ref):
    def emit(z, state):
        state_ref[z] = state

    half_state(rows, half_rows(slab, place()[3]), own, g_ref, r_ref, gp_ref, fwd_ref, last_ref, keep_ref, source_ref, emit)


def split_cols(tile):
    return [tile[:, c:c + 128] for c in range(0, tile.shape[-1], 128)]


def half_tiles(plane):
    return [split_cols(plane[t:t + 8]) for t in range(0, plane.shape[0], 8)]


def products(left, right):
    return [[x * y for x, y in zip(*lines)] for lines in zip(left, right)]


def put_tiles(ref, z, tiles):
    for t, line in enumerate(tiles):
        for c, tile in enumerate(line):
            ref[z, 8 * t:8 * t + 8, 128 * c:128 * c + 128] = tile


def explicit_tiles(state, s, vsum, ssum):
    return [[x + SECTION_RATE * w * (v - x * n) for x, w, v, n in zip(*lines)] for lines in zip(state, s, vsum, ssum)]


def own_explicit_kernel(
    rows, slab,
    own, s_ref, g_ref, r_ref, gp_ref, fwd_ref, last_ref, keep_ref, source_ref, ssum_ref,
    state_ref, part_ref,
):
    at = half_rows(slab, place()[3])

    def emit(z, state):
        state_ref[z] = state
        state, s = half_tiles(state), half_tiles(s_ref[z, at])
        put_tiles(part_ref, z, explicit_tiles(state, s, neighbour_sum(products(s, state)), half_tiles(ssum_ref[z, at])))

    half_state(rows, at, own, g_ref, r_ref, gp_ref, fwd_ref, last_ref, keep_ref, source_ref, emit)


def middle_kernel(
    rows, slab, cols,
    own, other, state_own, part_own, s_ref, g_ref, r_ref, gp_ref, fwd_in, last_ref, keep_ref, source_ref, ssum_ref,
    border_ref, reaction_lo, reaction_hi,
    e_own, fwd_ref, send_ref,
    e_other,
):
    row = lax.broadcasted_iota(jnp.int32, (8, cols), 0)
    half = place()[3]
    second = half == 1
    low_tile, high_tile = jnp.where(second, other[4], own[4]), jnp.where(second, own[4], other[4])
    inflow_b = jnp.where(row == 7, low_tile[0:1], high_tile[0:1])
    border = [jnp.where(row == 7, low_tile[1:2], high_tile[1:2])]
    narrow = lax.broadcasted_iota(jnp.int32, (8, 128), 0)
    bottom = narrow == 7
    mine, at = half_rows(slab, half), half_rows(slab, 1 - half)

    def around(is_second, flow_b, neighbour):
        return [jnp.where(is_second, jnp.where(bottom, high, b), jnp.where(bottom, b, low))
                for b, low, high in zip(flow_b, neighbour[0], neighbour[1])]

    def border_part(is_second, tile):
        return [jnp.where(is_second, jnp.where(bottom, 0.0, x), jnp.where(bottom, x, 0.0)) for x in tile]

    def to_rows(tile):
        return ([jnp.where(narrow == 0, pltpu.roll(x, 1, 0), 0.0) for x in tile],
                [jnp.where(narrow == 7, pltpu.roll(x, 7, 0), 0.0) for x in tile])

    def explicit(z, new):
        sb, gb, rb, gpb, fb = [border_ref[k, z] for k in range(5)]
        keep_b, source_b = [jnp.where(row == 7, reaction_lo[k, z:z + 1], reaction_hi[k, z:z + 1]) for k in (0, 1)]
        rhs = fb + gpb * inflow_b
        ub = border[0] = rb * (rhs + border[0]) if z == rows - 1 else rb * rhs + gb * border[0]
        flow_b = split_cols(sb * (source_b + keep_b * ub))
        sb = split_cols(sb)
        kept, s_kept = half_tiles(state_own[z]), half_tiles(s_ref[z, mine])
        state, s = half_tiles(new), half_tiles(s_ref[z, at])
        flow_kept, flow = products(s_kept, kept), products(s, state)

        ssum = half_tiles(ssum_ref[z, at])
        ssum = [[x + y for x, y in zip(*lines)] for lines in zip(ssum, to_rows(border_part(half == 0, sb)))]
        vsum = neighbour_sum(flow, around(half == 0, flow_b, flow_kept))
        put_tiles(e_other, z, explicit_tiles(state, s, vsum, ssum))

        v_more, s_more = to_rows(around(second, flow_b, flow)), to_rows(border_part(second, sb))
        part = half_tiles(part_own[z])
        put_tiles(e_own, z, [
            [p + SECTION_RATE * w * (v - x * n) for p, w, v, x, n in zip(*lines)]
            for lines in zip(part, s_kept, v_more, kept, s_more)])

    half_state(rows, at, other, g_ref, r_ref, gp_ref, fwd_in, last_ref, keep_ref, source_ref, explicit)
    half_sweep(rows, at, lambda z: e_other[z], g_ref, r_ref, gp_ref, last_ref, fwd_ref, send_ref)


def second_own_kernel(rows, slab, e_ref, g_ref, r_ref, gp_ref, last_ref, fwd_ref, mine_ref):
    at = half_rows(slab, place()[3])
    half_sweep(rows, at, lambda z: e_ref[z], g_ref, r_ref, gp_ref, last_ref, fwd_ref, mine_ref)


def final_kernel(
    rows, slab,
    other, state_own, g_ref, r_ref, gp_ref, fwd_ref, last_ref, keep_ref, source_ref,
    out_hbm, out, sems, own_sem,
):
    half = place()[3]
    own_copy = pltpu.make_async_copy(state_own, out_hbm.at[:, half_rows(slab, half)], own_sem)
    own_copy.start()
    at = half_rows(slab, 1 - half)
    copies = []

    def emit(z, state):
        out[z] = state
        if z % CHUNK == 0:
            here = pl.ds(z, CHUNK)
            copy = pltpu.make_async_copy(out.at[here], out_hbm.at[here, at], sems.at[z // CHUNK])
            copy.start()
            copies.append(copy)

    half_state(rows, at, other, g_ref, r_ref, gp_ref, fwd_ref, last_ref, keep_ref, source_ref, emit)
    for copy in copies:
        copy.wait()
    own_copy.wait()


def on_device(partners, concentration, tissue_mask, wall_layer, stiffness, production, layer_diffusivity, uptake_rate):
    rows, slab, cols = concentration.shape
    nx, nax = lax.axis_size("xs"), lax.axis_size("ax")
    block = (rows, slab, cols)
    smem = pl.BlockSpec(memory_space=pltpu.SMEM)
    hbm = pl.BlockSpec(memory_space=pltpu.HBM)

    def in_hbm(x):
        return pltpu.with_memory_space_constraint(x, pltpu.HBM)

    def call(kernel, outs, operands, scratch=(), specs=None, out_specs=None, us=1.0):
        return pl.pallas_call(
            kernel,
            out_shape=outs,
            in_specs=specs or [vspec()] * len(operands),
            out_specs=out_specs or [vspec()] * len(outs),
            scratch_shapes=list(scratch),
            compiler_params=params(),
            cost_estimate=cost(us),
        )(*operands)

    def exchange(block, stage):
        received = {step: lax.ppermute(block, "ax", route) for step, route in partners[stage]}
        return [received[step] for step, _ in partners[stage]]

    def f32(*shape):
        return pltpu.VMEM(shape, jnp.float32)

    def i32(*shape):
        return pltpu.VMEM(shape, jnp.int32)

    conc, mask, layer, stiff = [
        in_hbm(x) for x in (concentration, tissue_mask, wall_layer, stiffness)]
    diff_table, uptake_rate = in_hbm(layer_diffusivity), in_hbm(uptake_rate)
    lo, hi, first_s = call(
        functools.partial(edge_kernel, slab, cols),
        [at_vmem(3, rows, cols), at_vmem(3, rows, cols), at_vmem(slab, cols)],
        [diff_table, conc, mask, layer, stiff],
        scratch=[i32(2, 2, rows, cols), i32(2, 2, rows, cols), f32(2, 4, rows, cols),
                 i32(slab, cols), i32(slab, cols), f32(slab, cols),
                 pltpu.SemaphoreType.DMA((2, 8)), pltpu.SemaphoreType.DMA((3,))],
        specs=[smem] + [hbm] * 4,
    )
    def from_neighbours(lo, hi):
        odd = lax.rem(lax.axis_index("xs"), 2) == 1
        first = lax.ppermute(jnp.where(odd, lo, hi), "xs", [(i, i ^ 1) for i in range(nx)])
        second = lax.ppermute(jnp.where(odd, hi, lo), "xs", [(i, nx - 1 - i) for i in range(nx)])
        return jnp.where(odd, first, second), jnp.where(odd, second, first)

    from_lo, from_hi = from_neighbours(lo, hi)
    above_s = lax.ppermute(first_s, "ax", [((i + 1) % nax, i) for i in range(nax)])

    s, g, r, gp, ssum, part, ends = call(
        functools.partial(setup_kernel, rows, slab, cols),
        [at_vmem(*block)] * 6 + [at_vmem(2, slab, cols)],
        [diff_table, concentration, tissue_mask, wall_layer, stiffness],
        specs=[smem] + [vspec()] * 4,
        us=5.0,
    )
    stack, pair = 2 * PLANES + 1, (5, 8, cols)
    half_block = (rows, slab // 2, cols)
    last, flux, fwd_other, send, border, own_border = call(
        functools.partial(first_forward_kernel, rows, slab, cols, nx, nax),
        [at_vmem(2, slab, cols), at_vmem(2, rows, cols), at_vmem(*half_block), at_vmem(stack, 8, cols),
         at_vmem(5, rows, 8, cols), at_vmem(8, cols)],
        [lo, hi, s, g, r, gp, part, ends, from_lo, from_hi, above_s],
        scratch=[f32(2, 8, cols), f32(2, 3, rows, cols)],
    )
    fwd_own, mine = call(
        functools.partial(first_own_kernel, rows, slab, cols),
        [at_vmem(*half_block), at_vmem(stack, 8, cols)],
        [g, r, gp, part, ends, flux, last, own_border],
    )

    levs, values, border_levs = [], [], []
    for stage in (0, 1):
        received = exchange(mine if stage else send, stage)
        joins = len(received)
        if stage == 1:
            uptake_late, mine = lax.optimization_barrier((uptake_rate, mine))
            keep, source, lo, hi = call(
                functools.partial(reaction_kernel, rows),
                [at_vmem(*block)] * 2 + [at_vmem(2, rows, cols)] * 2,
                [uptake_late, tissue_mask, wall_layer, production],
                specs=[smem] + [vspec()] * 3,
                us=2.0,
            )
            reaction_lo, reaction_hi = from_neighbours(lo, hi)
            mine, keep, source = lax.optimization_barrier((mine, keep, source))
        mine, lev, value, border_lev = call(
            functools.partial(first_join_kernel, stage, joins),
            [at_vmem(stack, 8, cols), at_vmem(2 * JOIN_COEFS * joins, 8, cols), at_vmem(4 * joins, 8, cols),
             at_vmem(joins, 8, cols)],
            [mine, *received],
        )
        levs.append(lev)
        values.append(value)
        border_levs.append(border_lev)
    received = exchange(mine, 2)
    joins = len(received)
    own, send, lev = call(
        functools.partial(first_last_kernel, joins),
        [at_vmem(*pair), at_vmem(*pair), at_vmem(2 * JOIN_COEFS * joins, 8, cols)],
        [mine, *received, *levs, *values, *border_levs],
        scratch=[f32(4 * joins, 8, cols), f32(joins, 8, cols)],
    )
    levs.append(lev)
    (other,) = exchange(send, 0)
    state_own, part_own = call(
        functools.partial(own_explicit_kernel, rows, slab),
        [at_vmem(*half_block)] * 2,
        [own, s, g, r, gp, fwd_own, last, keep, source, ssum],
    )
    e, fwd_other, send = call(
        functools.partial(middle_kernel, rows, slab, cols),
        [at_vmem(*half_block), at_vmem(*half_block), at_vmem(4, 8, cols)],
        [own, other, state_own, part_own, s, g, r, gp, fwd_other, last, keep, source, ssum, border,
         reaction_lo, reaction_hi],
        scratch=[f32(*half_block)],
        us=3.0,
    )
    fwd_own, mine = call(
        functools.partial(second_own_kernel, rows, slab),
        [at_vmem(*half_block), at_vmem(4, 8, cols)],
        [e, g, r, gp, last],
    )
    values = []
    for stage in (0, 1):
        received = exchange(mine if stage else send, stage)
        joins = len(received)
        mine, value = call(
            functools.partial(second_join_kernel, stage, joins),
            [at_vmem(4, 8, cols), at_vmem(4 * joins, 8, cols)],
            [mine, *received, levs[stage]],
        )
        values.append(value)
    received = exchange(mine, 2)
    joins = len(received)
    own, send = call(
        functools.partial(second_last_kernel, joins),
        [at_vmem(4, 8, cols), at_vmem(4, 8, cols)],
        [mine, *received, *levs, *values],
        scratch=[f32(4 * joins, 8, cols)],
    )
    (other,) = exchange(send, 0)
    (state_own,) = call(
        functools.partial(own_state_kernel, rows, slab),
        [at_vmem(*half_block)],
        [own, g, r, gp, fwd_own, last, keep, source],
    )
    (out,) = call(
        functools.partial(final_kernel, rows, slab),
        [jax.ShapeDtypeStruct(block, jnp.float32)],
        [other, state_own, g, r, gp, fwd_other, last, keep, source],
        scratch=[f32(*half_block), pltpu.SemaphoreType.DMA((rows // CHUNK,)), pltpu.SemaphoreType.DMA],
        out_specs=[hbm],
    )
    return out


def join_partners():
    stages = (
        ((1, lambda y, z, c: (y, z, 1 - c)),),
        tuple((k, lambda y, z, c, k=k: (y, z ^ k, c ^ (k & 1))) for k in ORDER),
        tuple((k, lambda y, z, c, k=k: (y ^ k, z, c ^ (k & 1))) for k in ORDER),
    )
    routes = []
    for flips in stages:
        routes.append([])
        for step, flip in flips:
            route = []
            for i in range(32):
                y, z, c = flip(i // 8, i // 2 % 4, i % 2)
                route.append((i, y * 8 + z * 2 + c))
            routes[-1].append((step, route))
    return routes


def solution(mesh):
    placed = (P("ax", "xs", None),) * 5 + (P(), P())
    return jax.shard_map(
        functools.partial(on_device, join_partners()),
        mesh=mesh, in_specs=placed, out_specs=P("ax", "xs", None), check_vma=False,
    )
```
